128 devices in a mesh: gx: 8 (over z, core), gy: 16 (over y, x).
Axes of the slice: x: 4, y: 4, z: 4, core: 2. Of those that a mesh axis runs over, the one named last changes fastest.
Arguments:
- residual: float32 [4, 96, 192, 384], P(None, 'gx', 'gy'), may hold values from -6 to 6
- sx_block: float32 [16, 8, 8], P('gx'), may hold values from -2 to 2
- sy_block: float32 [32, 8, 8], P('gy'), may hold values from -2 to 2
- depth_eigenvectors: float32 [64, 8, 8], replicated, may hold values from -2 to 2
- lam_x: float32 [16, 8], P('gx'), may hold values from 0.1 to 2
- lam_y: float32 [32, 8], P('gy'), may hold values from 0.1 to 2
- depth_eigenvalues: float32 [64, 8], replicated, may hold values from 0.1 to 2
- coarse_factor: bfloat16 [8, 16, 585, 7233], P('gx', 'gy'), may hold values from -0.1504 to 0.1504, as said below
Outputs:
- preconditioned: float32 [4, 96, 192, 384], P(None, 'gx', 'gy')
The draws below stay inside these ranges and needn't reach their ends.
Inputs may be any that keep to these rules, and one draw needn't show every extreme that they name: `coarse_factor`: block [gx, gy] holds the rows of that device's (3) (3) (65) local vertices. A vertex held by several devices (on block boundaries, periodically) has the same row on each of them; such a row is zero in the own columns and in the columns of every tree level below the lowest level whose node contains all devices that hold the vertex. A vertex held by one device has no such zeros.
All inputs are finite; a program needn't handle non-finite values.
Results may differ from the reference program's by a relative error of at most 0.00045.
Values sent between devices are 32-bit elements; how exact they have to be, the bound alone decides.
No kernel may reach another device: no remote copies, remote signals or barrier semaphores. Data moves between devices by JAX's collectives and lax.ppermute only.
A program may use at most 128 MiB of HBM per device.

```python
import math
import jax
import jax.numpy as jnp
import numpy as np
from jax import lax

PRESSURE_POINTS = 6
EX = 2
EY = 2
EZ = 64
NRHS = 4
SEP = 1024
NEX = 16
NEY = 32
ELEMENTS_DEPTH = 64
NX = 96
NY = 192
NZ = 384
LEAF = 65
VLOC = 585
LEVELS = 7
COLS = 7233


def draw_coarse_factor(key, part):
    grid_x = NEX // EX
    grid_y = NEY // EY
    vertex_span = EZ + 1
    vertex_table = jax.random.normal(key, (NEX * NEY * vertex_span, COLS), jnp.float32)
    vertex_table = (jnp.clip(vertex_table, -5.0, 5.0) * 0.03).astype(jnp.bfloat16)
    dev_x = jnp.arange(grid_x, dtype=jnp.int32)[:, None, None, None, None]
    dev_y = jnp.arange(grid_y, dtype=jnp.int32)[None, :, None, None, None]
    vert_a = jnp.arange(EX + 1, dtype=jnp.int32)[None, None, :, None, None]
    vert_b = jnp.arange(EY + 1, dtype=jnp.int32)[None, None, None, :, None]
    vertex_third = jnp.arange(vertex_span, dtype=jnp.int32)[None, None, None, None, :]
    global_x = (dev_x * EX + vert_a) % NEX
    global_y = (dev_y * EY + vert_b) % NEY
    vertex_ids = (global_x * NEY + global_y) * vertex_span + vertex_third
    spread_x = jnp.bitwise_or(jnp.where(vert_a == 0, jnp.bitwise_xor(dev_x, (dev_x - 1) % grid_x), 0), jnp.where(vert_a == EX, jnp.bitwise_xor(dev_x, (dev_x + 1) % grid_x), 0))
    spread_y = jnp.bitwise_or(jnp.where(vert_b == 0, jnp.bitwise_xor(dev_y, (dev_y - 1) % grid_y), 0), jnp.where(vert_b == EY, jnp.bitwise_xor(dev_y, (dev_y + 1) % grid_y), 0))
    spread = jnp.bitwise_or(spread_x * grid_y, spread_y)
    home_level = jnp.zeros(spread.shape, jnp.int32)
    for level_bit in range(LEVELS):
        home_level = home_level + (spread >= 1 << level_bit).astype(jnp.int32)
    home_level = jnp.broadcast_to(home_level, (grid_x, grid_y, EX + 1, EY + 1, vertex_span))
    home_level = home_level.reshape(grid_x, grid_y, VLOC, 1)
    column = jnp.arange(COLS, dtype=jnp.int32)
    column_level = jnp.where(column < LEAF, 0, 1 + (column - LEAF) // SEP)
    keep_mask = jnp.where(column < LEAF, home_level == 0, column_level >= home_level)
    flat_ids = jnp.broadcast_to(vertex_ids, (grid_x, grid_y, EX + 1, EY + 1, vertex_span)).reshape(grid_x, grid_y, VLOC)
    values = vertex_table[flat_ids]
    return jnp.where(keep_mask, values, jnp.zeros((), jnp.bfloat16))


def block_scale(stream_key, shape, split, smallest, top_value):
    def one(dim, parts):
        draws = jax.random.uniform(jax.random.fold_in(jax.random.fold_in(stream_key, 6), dim), (parts,), jnp.float32, smallest / len(split), top_value / len(split))
        return jnp.repeat(jnp.exp(draws), shape[dim] // parts).reshape((-1,) + (1,) * (len(shape) - dim - 1))

    loudness = one(*split[0])
    for cut in split[1:]:
        loudness = loudness * one(*cut)
    return loudness


def gaussian(own_key, dims, scale, limit, split=(), held_as=jnp.bfloat16):
    values = jax.random.normal(own_key, dims, jnp.float32) * scale
    if len(split) > 0:
        values = block_scale(own_key, dims, split, -0.22, 0.18) * values
    return jnp.clip(values, min=-limit, max=limit).astype(held_as)


def setup_inputs(seed: int = 0) -> dict:
    arg_keys = jax.random.split(jax.random.key(seed), 9)
    residual = gaussian(arg_keys[0], (NRHS, NX, NY, NZ), 1.0, 6.0, ((1, 8), (2, 16)), jnp.float32)
    sx_block = gaussian(arg_keys[1], (NEX, PRESSURE_POINTS + 2, PRESSURE_POINTS + 2), (PRESSURE_POINTS + 2) ** -0.5, 2.0, ((0, 8),), jnp.float32)
    sy_block = gaussian(arg_keys[2], (NEY, PRESSURE_POINTS + 2, PRESSURE_POINTS + 2), (PRESSURE_POINTS + 2) ** -0.5, 2.0, ((0, 16),), jnp.float32)
    depth_eigenvectors = gaussian(arg_keys[3], (ELEMENTS_DEPTH, PRESSURE_POINTS + 2, PRESSURE_POINTS + 2), (PRESSURE_POINTS + 2) ** -0.5, 2.0, (), jnp.float32)
    lam_x = jnp.clip(jnp.exp(math.log(2.0) - 2.9957323 * jax.random.uniform(arg_keys[4], (NEX, PRESSURE_POINTS + 2), jnp.float32) ** block_scale(arg_keys[4], (NEX, PRESSURE_POINTS + 2), ((0, 8),), -0.2, 0.2)), 0.1, 2.0)
    lam_y = jnp.clip(jnp.exp(math.log(2.0) - 2.9957323 * jax.random.uniform(arg_keys[5], (NEY, PRESSURE_POINTS + 2), jnp.float32) ** block_scale(arg_keys[5], (NEY, PRESSURE_POINTS + 2), ((0, 16),), -0.2, 0.2)), 0.1, 2.0)
    depth_eigenvalues = jnp.clip(jnp.exp(jax.random.uniform(arg_keys[6], (ELEMENTS_DEPTH, PRESSURE_POINTS + 2), jnp.float32, math.log(0.1), math.log(2.0))), 0.1, 2.0)
    coarse_factor = draw_coarse_factor(jax.random.fold_in(arg_keys[8], 71), 0)
    return {"residual": residual, "sx_block": sx_block, "sy_block": sy_block, "depth_eigenvectors": depth_eigenvectors, "lam_x": lam_x, "lam_y": lam_y, "depth_eigenvalues": depth_eigenvalues, "coarse_factor": coarse_factor}


exact_mode = lax.Precision.HIGHEST

gauss_nodes = [-0.93246951420315205, -0.66120938646626451, -0.23861918608319691,
               0.23861918608319691, 0.66120938646626451, 0.93246951420315205]
gauss_weights = [0.17132449237917034, 0.36076157304813861, 0.46791393457269105,
                 0.46791393457269105, 0.36076157304813861, 0.17132449237917034]


def hat_tables(point_count):
    nodes = np.array(gauss_nodes)
    weights = np.array(gauss_weights)
    prolong = np.stack([(1.0 - nodes) / 2.0, (1.0 + nodes) / 2.0])
    restrict = prolong * weights[None, :]
    return jnp.asarray(restrict, jnp.float32), jnp.asarray(prolong, jnp.float32)


def element_boxes(padded, axis_pos, elem_count, point_count):
    extra_cells = (elem_count + 1) * point_count - padded.shape[axis_pos]
    width_list = [(0, 0)] * padded.ndim
    width_list[axis_pos] = (0, extra_cells)
    grown_field = jnp.pad(padded, width_list)
    new_shape = grown_field.shape[:axis_pos] + (elem_count + 1, point_count) + grown_field.shape[axis_pos + 1:]
    blocks = grown_field.reshape(new_shape)
    head_part = lax.slice_in_dim(blocks, 0, elem_count, axis=axis_pos)
    tail_part = lax.slice_in_dim(lax.slice_in_dim(blocks, 1, elem_count + 1, axis=axis_pos), 0, 2, axis=axis_pos + 1)
    return jnp.concatenate([head_part, tail_part], axis=axis_pos + 1)


def fast_solve(element_box, sx_block, sy_block, depth_eigenvectors, lam_x, lam_y, depth_eigenvalues):
    transformed = jnp.einsum('naubvcw,aup->napbvcw', element_box, sx_block, precision=exact_mode)
    transformed = jnp.einsum('napbvcw,bvq->napbqcw', transformed, sy_block, precision=exact_mode)
    transformed = jnp.einsum('napbqcw,cwr->napbqcr', transformed, depth_eigenvectors, precision=exact_mode)
    spectrum = (lam_x[:, :, None, None, None, None] + lam_y[None, None, :, :, None, None]
                + depth_eigenvalues[None, None, None, None, :, :])
    transformed = transformed / spectrum[None]
    restored = jnp.einsum('napbqcr,aup->naubqcr', transformed, sx_block, precision=exact_mode)
    restored = jnp.einsum('naubqcr,bvq->naubvcr', restored, sy_block, precision=exact_mode)
    restored = jnp.einsum('naubvcr,cwr->naubvcw', restored, depth_eigenvectors, precision=exact_mode)
    return restored


def schwarz_part(padded, sx_block, sy_block, depth_eigenvectors, lam_x, lam_y, depth_eigenvalues, point_count):
    elem_x = sx_block.shape[0]
    elem_y = sy_block.shape[0]
    elem_z = depth_eigenvectors.shape[0]
    element_box = element_boxes(padded, 1, elem_x, point_count)
    element_box = element_boxes(element_box, 3, elem_y, point_count)
    element_box = element_boxes(element_box, 5, elem_z, point_count)
    solved = fast_solve(element_box, sx_block, sy_block, depth_eigenvectors, lam_x, lam_y, depth_eigenvalues)
    inner_part = solved[:, :, 1:point_count + 1, :, 1:point_count + 1, :, 1:point_count + 1]
    rhs_count = inner_part.shape[0]
    return inner_part.reshape(rhs_count, elem_x * point_count, elem_y * point_count, elem_z * point_count)


def corner_sum(corner_terms, axis_pos):
    first_corner = lax.index_in_dim(corner_terms, 0, axis_pos + 1, keepdims=False)
    second_corner = lax.index_in_dim(corner_terms, 1, axis_pos + 1, keepdims=False)
    widths_end = [(0, 0)] * first_corner.ndim
    widths_end[axis_pos] = (0, 1)
    widths_front = [(0, 0)] * first_corner.ndim
    widths_front[axis_pos] = (1, 0)
    return jnp.pad(first_corner, widths_end) + jnp.pad(second_corner, widths_front)


def restrict_vertices(field_row_block, restrict, elem_x, elem_y, elem_z, point_count):
    rhs_count = field_row_block.shape[0]
    point_cells = field_row_block.reshape(rhs_count, elem_x, point_count, elem_y, point_count, elem_z, point_count)
    corner_terms = jnp.einsum('naibjck,si->nasbjck', point_cells, restrict, precision=exact_mode)
    corner_terms = jnp.einsum('nasbjck,tj->nasbtck', corner_terms, restrict, precision=exact_mode)
    corner_terms = jnp.einsum('nasbtck,uk->nasbtcu', corner_terms, restrict, precision=exact_mode)
    corner_terms = corner_sum(corner_terms, 1)
    corner_terms = corner_sum(corner_terms, 2)
    corner_terms = corner_sum(corner_terms, 3)
    return corner_terms.reshape(rhs_count, -1)


def corner_pairs(vertex_grid, axis_pos):
    size_along = vertex_grid.shape[axis_pos]
    low_side = lax.slice_in_dim(vertex_grid, 0, size_along - 1, axis=axis_pos)
    high_side = lax.slice_in_dim(vertex_grid, 1, size_along, axis=axis_pos)
    return jnp.stack([low_side, high_side], axis=axis_pos + 1)


def prolong_points(vertex_rows, prolong, elem_x, elem_y, elem_z, point_count):
    rhs_count = vertex_rows.shape[0]
    vertex_grid = vertex_rows.reshape(rhs_count, elem_x + 1, elem_y + 1, elem_z + 1)
    vertex_grid = corner_pairs(vertex_grid, 1)
    vertex_grid = jnp.einsum('nasyz,si->naiyz', vertex_grid, prolong, precision=exact_mode)
    vertex_grid = corner_pairs(vertex_grid, 3)
    vertex_grid = jnp.einsum('naibtz,tj->naibjz', vertex_grid, prolong, precision=exact_mode)
    vertex_grid = corner_pairs(vertex_grid, 5)
    vertex_grid = jnp.einsum('naibjcu,uk->naibjck', vertex_grid, prolong, precision=exact_mode)
    return vertex_grid.reshape(rhs_count, elem_x * point_count, elem_y * point_count, elem_z * point_count)


def reference(residual, sx_block, sy_block, depth_eigenvectors, lam_x, lam_y, depth_eigenvalues, coarse_factor):
    restrict, prolong = hat_tables(PRESSURE_POINTS)
    grid_x = coarse_factor.shape[0]
    grid_y = coarse_factor.shape[1]
    devices = grid_x * grid_y
    span_x = NX // grid_x
    span_y = NY // grid_y

    def device_blocks(field):
        return field.reshape(grid_x, span_x, grid_y, span_y, NZ).transpose(0, 2, 1, 3, 4).reshape(devices, span_x, span_y, NZ)

    def first_section(field):
        wrapped = jnp.pad(field, ((1, 1), (1, 1), (0, 0)), mode="wrap")
        padded = jnp.pad(wrapped, ((0, 0), (0, 0), (1, 1)))
        local_portion = schwarz_part(padded[None], sx_block, sy_block, depth_eigenvectors, lam_x, lam_y, depth_eigenvalues, PRESSURE_POINTS)[0]
        vertex_terms = restrict_vertices(device_blocks(field), restrict, EX, EY, EZ, PRESSURE_POINTS)
        return local_portion, vertex_terms

    local_parts, vertex_terms = lax.map(first_section, residual)
    rounded = vertex_terms.astype(jnp.bfloat16).transpose(1, 0, 2)
    factor_rows = coarse_factor.reshape(devices, VLOC, COLS)
    partial_value = lax.map(lambda operands: jnp.dot(operands[0], operands[1], preferred_element_type=jnp.float32),
                      (rounded, factor_rows))
    rhs_count = partial_value.shape[1]
    pieces = [partial_value[:, :, :LEAF]]
    for level_index in range(1, LEVELS + 1):
        level_block = partial_value[:, :, LEAF + (level_index - 1) * SEP:LEAF + level_index * SEP]
        group_size = 2 ** level_index
        summed = level_block.reshape(devices // group_size, group_size, rhs_count, SEP).sum(axis=1)
        pieces.append(jnp.repeat(summed, group_size, axis=0))
    node_values = jnp.concatenate(pieces, axis=2).astype(jnp.bfloat16)
    vertex_values = lax.map(
        lambda operands: lax.dot_general(operands[0], operands[1], (((1,), (1,)), ((), ())),
                                         preferred_element_type=jnp.float32),
        (node_values, factor_rows))
    vertex_values = vertex_values.transpose(1, 0, 2)

    def second_section(operands):
        local_portion, vertex_rows = operands
        coarse_blocks = prolong_points(vertex_rows, prolong, EX, EY, EZ, PRESSURE_POINTS)
        coarse_field = coarse_blocks.reshape(grid_x, grid_y, span_x, span_y, NZ).transpose(0, 2, 1, 3, 4).reshape(NX, NY, NZ)
        return local_portion + coarse_field

    return lax.map(second_section, (local_parts, vertex_values))
```

```python
import jax
import jax.numpy as jnp
import numpy as np
import ml_dtypes
from jax import lax
from jax.experimental import pallas as pl
from jax.experimental.pallas import tpu as pltpu
from jax.sharding import PartitionSpec as P

SEP = 1024
LEAF = 65
LEVELS = 7
VLOC = 585
COLS = 7233
WIDE = 8192
BF = jnp.bfloat16
F32 = jnp.float32

gauss_nodes = [
    -0.932469514203152,
    -0.6612093864662645,
    -0.2386191860831969,
    0.2386191860831969,
    0.6612093864662645,
    0.932469514203152,
]
gauss_weights = [
    0.17132449237917033,
    0.3607615730481386,
    0.46791393457269104,
    0.46791393457269104,
    0.3607615730481386,
    0.17132449237917033,
]
prolong_np = np.stack(
    [(1.0 - np.array(gauss_nodes)) / 2.0, (1.0 + np.array(gauss_nodes)) / 2.0]
).astype(np.float32)
restrict_np = (
    np.stack([(1.0 - np.array(gauss_nodes)) / 2.0, (1.0 + np.array(gauss_nodes)) / 2.0])
    * np.array(gauss_weights)[None, :]
).astype(np.float32)


def line_table(table, elems):
    out = np.zeros((elems * 6, elems + 1), np.float32)
    for c in range(elems):
        for k in range(6):
            out[6 * c + k, c] = table[0, k]
            out[6 * c + k, c + 1] = table[1, k]
    return out


def split_np(x):
    hi = x.astype(ml_dtypes.bfloat16)
    lo = (x - hi.astype(np.float32)).astype(ml_dtypes.bfloat16)
    return hi, lo


def split(x):
    hi = x.astype(BF)
    lo = (x - hi.astype(F32)).astype(BF)
    return hi, lo


def dot(a, b, dims=(((1,), (0,)), ((), ()))):
    return lax.dot_general(a, b, dims, preferred_element_type=F32)


NT = (((1,), (1,)), ((), ()))
TN = (((0,), (0,)), ((), ()))


def dot3(a, b, dims=(((1,), (0,)), ((), ()))):
    return dot(a[0], b[0], dims) + (dot(a[0], b[1], dims) + dot(a[1], b[0], dims))


def ab_mask(rows, cols):
    col = lax.broadcasted_iota(jnp.int32, (rows, cols), 1)
    ab = lax.broadcasted_iota(jnp.int32, (rows, cols), 0) // 8
    return jnp.logical_and(col >= ab * 65, col < ab * 65 + 65)


FACE = 12 * 384
SLAB = 14 * 384
CUT = 5120
TAIL = COLS - CUT
TAIL_WIDE = 2176
PADDED = 7296
BIG = 51 << 20
ROW_CHUNKS = ((512, 73), (0, 256), (256, 128), (384, 128))
SMALL = 24 << 20
HBM = pl.BlockSpec(memory_space=pltpu.HBM)
UNUSED = pl.BlockSpec(memory_space=pl.ANY)


def whole(shape):
    return pl.BlockSpec(shape, lambda i: (0,) * len(shape))


def parities():
    return lax.axis_index("gy") % 2 == 1, lax.axis_index("gx") % 2 == 1


def forward_kernel(
    r_hbm, rz_hbm, tile_hbm, f_ref,
    msg_ref, own_ref, y2_ref, x1_ref, x2_ref, keep_ref,
    r_ref, rz_ref, tile_ref, u_ref, acc_ref, small_sems, sems,
):
    small = []
    for k, (src, dst) in enumerate(((r_hbm, r_ref), (rz_hbm, rz_ref), (tile_hbm, tile_ref))):
        small.append(pltpu.make_async_copy(src, dst, small_sems.at[k]))
        small[-1].start()
    copies = []
    for k, (start, size) in enumerate(ROW_CHUNKS):
        rows = pl.ds(start, size)
        copies.append(pltpu.make_async_copy(f_ref.at[rows, :], keep_ref.at[rows, :], sems.at[k]))
        copies[-1].start()

    u_ref[...] = jnp.zeros_like(u_ref)
    small[0].wait()
    r0 = [float(v) for v in restrict_np[0]]
    r1 = [float(v) for v in restrict_np[1]]
    for y_elem in range(2):
        sums = []
        for j in range(6):
            y = 6 * y_elem + j
            lows = [r_ref[i, y] for i in range(6)]
            highs = [r_ref[6 + i, y] for i in range(6)]
            sums.append(
                [
                    sum(r0[i] * lows[i] for i in range(6)),
                    sum(r1[i] * lows[i] for i in range(6)) + sum(r0[i] * highs[i] for i in range(6)),
                    sum(r1[i] * highs[i] for i in range(6)),
                ]
            )
        for a in range(3):
            for t, table in ((0, r0), (1, r1)):
                row = (a * 3 + y_elem + t) * 8
                u_ref[row : row + 4, :] += sum(table[j] * sums[j][a] for j in range(6))
    small[1].wait()
    vert = dot3(split(u_ref[...]), (rz_ref[0], rz_ref[1])).astype(BF)
    small[2].wait()
    spread = dot(vert, tile_ref[...])
    spread = jnp.where(ab_mask(72, 640), spread, 0.0)
    v = sum(spread[8 * k : 8 * k + 8] for k in range(9)).astype(BF)[:, :VLOC]

    gy_odd, gx_odd = parities()
    for i in range(12):
        cols = slice(384 * i, 384 * i + 384)
        low, high = r_ref[i, 0], r_ref[i, 11]
        msg_ref[:, LEVELS * SEP + 384 * i : LEVELS * SEP + 384 * i + 384] = jnp.where(gy_odd, low, high)
        y2_ref[:, cols] = jnp.where(gy_odd, high, low)
        low, high = r_ref[0, i], r_ref[11, i]
        x1_ref[:, cols] = jnp.where(gx_odd, low, high)
        x2_ref[:, cols] = jnp.where(gx_odd, high, low)

    acc_ref[:, LEVELS * SEP :] = jnp.zeros((8, 128), F32)
    for k, (start, size) in enumerate(ROW_CHUNKS):
        copies[k].wait()
        rows = slice(start, start + size)
        product = dot(v[:, rows], keep_ref[rows, :])
        acc_ref[:, :COLS] = product if k == 0 else acc_ref[:, :COLS] + product
    own_ref[...] = acc_ref[:4, :128]
    msg_ref[:, : LEVELS * SEP] = pltpu.roll(acc_ref[...], PADDED - LEAF, 1)[:4, : LEVELS * SEP]


def forward(field, factor):
    rz = np.zeros((384, 128), np.float32)
    rz[:, :65] = line_table(restrict_np, 64)
    tile = np.zeros((128, 640), ml_dtypes.bfloat16)
    for ab in range(9):
        for c in range(65):
            tile[c, ab * 65 + c] = 1
    shapes = [(4, LEVELS * SEP + FACE), (4, 128), (4, FACE), (4, FACE), (4, FACE)]
    vm = pl.BlockSpec(memory_space=pltpu.VMEM)
    return pl.pallas_call(
        forward_kernel,
        in_specs=[HBM] * 4,
        out_specs=[vm] * 6,
        out_shape=[jax.ShapeDtypeStruct(v, F32) for v in shapes] + [jax.ShapeDtypeStruct((VLOC, COLS), BF)],
        scratch_shapes=[
            pltpu.VMEM((12, 12, 4, 384), F32),
            pltpu.VMEM((2, 384, 128), BF),
            pltpu.VMEM((128, 640), BF),
            pltpu.VMEM((72, 384), F32),
            pltpu.VMEM((8, PADDED), F32),
            pltpu.SemaphoreType.DMA((3,)),
            pltpu.SemaphoreType.DMA((len(ROW_CHUNKS),)),
        ],
        compiler_params=pltpu.CompilerParams(vmem_limit_bytes=BIG),
        cost_estimate=pl.CostEstimate(flops=2 * 8 * VLOC * COLS, bytes_accessed=9_500_000, transcendentals=0),
        name="forward",
    )(field, jnp.stack([jnp.asarray(v) for v in split_np(rz)]), jnp.asarray(tile), factor)


def faces_kernel(wait_ref, x1_ref, x2_ref, y1_ref, y2_ref, m1_ref, m2_ref):
    gy_odd, gx_odd = parities()
    m1_ref[:, :FACE] = x1_ref[...]
    m2_ref[:, :FACE] = x2_ref[...]
    tail = LEVELS * SEP
    low_x = slice(0, 384)
    high_x = slice(FACE - 384, FACE)

    def corner(cols):
        one = y1_ref[:, tail + cols.start : tail + cols.stop]
        two = y2_ref[:, cols]
        return jnp.where(gy_odd, one, two), jnp.where(gy_odd, two, one)

    low, high = corner(low_x), corner(high_x)
    for k in range(2):
        cols = slice(FACE + 384 * k, FACE + 384 * k + 384)
        m1_ref[:, cols] = jnp.where(gx_odd, low[k], high[k])
        m2_ref[:, cols] = jnp.where(gx_odd, high[k], low[k])


def faces(wait, x1, x2, y1, y2):
    vm = pl.BlockSpec(memory_space=pltpu.VMEM)
    return pl.pallas_call(
        faces_kernel,
        in_specs=[UNUSED] + [vm] * 4,
        out_specs=[vm] * 2,
        out_shape=[jax.ShapeDtypeStruct((4, SLAB), F32)] * 2,
        compiler_params=pltpu.CompilerParams(vmem_limit_bytes=SMALL),
        cost_estimate=pl.CostEstimate(flops=100_000, bytes_accessed=300_000, transcendentals=0),
        name="faces",
    )(wait, x1, x2, y1, y2)


def tables_kernel(wait_ref, sx_ref, sy_ref, dt_ref, lx_ref, ly_ref, lz_ref, a_ref, b_ref, zf_ref, zb_ref, rs_ref):
    lane = lax.broadcasted_iota(jnp.int32, (8, 256), 1)
    sub = lax.broadcasted_iota(jnp.int32, (8, 256), 0)
    slab = lane // 16
    xpos = jnp.where(slab < 12, slab + 1, jnp.where(slab == 12, 0, jnp.where(slab == 13, 13, 99)))
    yrow = lane % 16
    ypos = jnp.where(yrow < 12, yrow + 1, jnp.where(yrow == 12, 0, jnp.where(yrow == 13, 13, 99)))
    inner = jnp.logical_and(sub >= 1, sub <= 6)

    def exact(a, b, dims):
        return lax.dot_general(a, b, dims, precision=lax.Precision.HIGHEST, preferred_element_type=F32)

    def expand(mat_ref, pos, keep):
        parts = []
        for e in range(2):
            pick = jnp.where(jnp.logical_and(pos == 6 * e + sub, keep), 1.0, 0.0)
            parts.append(exact(mat_ref[e], pick, TN))
        return jnp.concatenate(parts, axis=0)

    everything = sub >= 0
    ax = expand(sx_ref, xpos, everything)
    ay = expand(sy_ref, ypos, everything)
    for i in range(16):
        hi, lo = split(ax[i : i + 1, :] * ay)
        a_ref[0, 16 * i : 16 * i + 16, :] = hi
        a_ref[1, 16 * i : 16 * i + 16, :] = lo
    bx = expand(sx_ref, xpos, inner)
    by = expand(sy_ref, ypos, inner)
    full = jnp.concatenate([bx[i : i + 1, :] * by for i in range(16)], axis=0)
    hi, lo = split(full.T)
    b_ref[0] = hi
    b_ref[1] = lo

    row = lax.broadcasted_iota(jnp.int32, (256, 8), 0)
    col = lax.broadcasted_iota(jnp.int32, (256, 8), 1)

    def column(lam_ref, group):
        total = jnp.zeros((256, 8), F32)
        for e in range(2):
            total += jnp.where(group == 8 * e + col, lam_ref[e : e + 1, :], 0.0)
        return jnp.sum(total, axis=1, keepdims=True)

    lateral = column(lx_ref, row // 16) + column(ly_ref, row % 16)

    for g in range(2):
        pick = jnp.where(
            lax.broadcasted_iota(jnp.int32, (64, 256), 0)
            == lax.broadcasted_iota(jnp.int32, (64, 256), 1) // 8 + 32 * g,
            1.0,
            0.0,
        )
        mine = sub == lane % 8
        spread = exact(dt_ref[...], pick, (((1,), (0,)), ((), ())))
        depth = exact(lz_ref[...], pick, (((1,), (0,)), ((), ())))
        depth = jnp.sum(jnp.where(mine, depth, 0.0), axis=0, keepdims=True)
        rs_ref[:, 256 * g : 256 * g + 256] = 1.0 / (lateral + depth)
        z = lax.broadcasted_iota(jnp.int32, (256, 256), 0) + 128 * g
        c = lax.broadcasted_iota(jnp.int32, (256, 256), 1) // 8 + 32 * g
        w = z + 1 - 6 * c
        table = jnp.zeros((256, 256), F32)
        for k in range(8):
            line = jnp.sum(jnp.where(mine, spread[8 * k : 8 * k + 8], 0.0), axis=0, keepdims=True)
            table = jnp.where(w == k, line, table)
        hi, lo = split(table)
        zf_ref[0, g] = hi
        zf_ref[1, g] = lo
        mid = jnp.logical_and(w >= 1, w <= 6)
        zb_ref[0, g] = jnp.where(mid, hi.astype(F32), 0.0).astype(BF)
        zb_ref[1, g] = jnp.where(mid, lo.astype(F32), 0.0).astype(BF)


def tables(wait, sx, sy, dt, lx, ly, lz):
    vm = pl.BlockSpec(memory_space=pltpu.VMEM)
    return pl.pallas_call(
        tables_kernel,
        in_specs=[UNUSED] + [vm] * 6,
        out_specs=[vm] * 5,
        out_shape=[
            jax.ShapeDtypeStruct((2, 256, 256), BF),
            jax.ShapeDtypeStruct((2, 256, 256), BF),
            jax.ShapeDtypeStruct((2, 2, 256, 256), BF),
            jax.ShapeDtypeStruct((2, 2, 256, 256), BF),
            jax.ShapeDtypeStruct((256, 512), F32),
        ],
        compiler_params=pltpu.CompilerParams(vmem_limit_bytes=SMALL),
        cost_estimate=pl.CostEstimate(flops=1_000_000_000, bytes_accessed=2_000_000, transcendentals=0),
        name="tables",
    )(wait, sx, sy, dt, lx, ly, lz)


def schwarz_kernel(
    first, wait_ref, r_ref, y1_ref, y2_ref, m1_ref, m2_ref, a_ref, b_ref, zf_ref, zb_ref, rs_ref, out_ref, x_ref
):
    gy_odd, gx_odd = parities()
    tail = LEVELS * SEP
    x_ref[...] = jnp.zeros_like(x_ref)
    for k in range(out_ref.shape[0]):
        n = first + k
        for x in range(12):
            x_ref[k, 16 * x : 16 * x + 12, :] = r_ref[x, :, n, :]
            one = y1_ref[n : n + 1, tail + 384 * x : tail + 384 * x + 384]
            two = y2_ref[n : n + 1, 384 * x : 384 * x + 384]
            x_ref[k, 16 * x + 12 : 16 * x + 13, :] = jnp.where(gy_odd, one, two)
            x_ref[k, 16 * x + 13 : 16 * x + 14, :] = jnp.where(gy_odd, two, one)
        for j in range(14):
            one = m1_ref[n : n + 1, 384 * j : 384 * j + 384]
            two = m2_ref[n : n + 1, 384 * j : 384 * j + 384]
            x_ref[k, 192 + j : 193 + j, :] = jnp.where(gx_odd, one, two)
            x_ref[k, 208 + j : 209 + j, :] = jnp.where(gx_odd, two, one)
        a = (a_ref[0][:, :224], a_ref[1][:, :224])
        t1 = split(dot3(a, split(x_ref[k])))
        backs = []
        for g in range(2):
            part = (t1[0][:, 128 * g : 128 * g + 256], t1[1][:, 128 * g : 128 * g + 256])
            t2 = dot3(part, (zf_ref[0, g], zf_ref[1, g]))
            t3 = split(t2 * rs_ref[:, 256 * g : 256 * g + 256])
            backs.append(dot3(t3, (zb_ref[0, g], zb_ref[1, g]), NT))
        t4 = split(
            jnp.concatenate(
                [backs[0][:, :128], backs[0][:, 128:] + backs[1][:, :128], backs[1][:, 128:]], axis=1
            )
        )
        out_ref[k] = dot3((b_ref[0][:192], b_ref[1][:192]), t4)


def schwarz(first, count, wait, field, y1, y2, m1, m2, tabs):
    vm = pl.BlockSpec(memory_space=pltpu.VMEM)
    kernel = lambda *refs: schwarz_kernel(first, *refs)
    return pl.pallas_call(
        kernel,
        in_specs=[UNUSED] + [vm] * 10,
        out_specs=vm,
        out_shape=jax.ShapeDtypeStruct((count, 192, 384), F32),
        scratch_shapes=[pltpu.VMEM((count, 224, 384), F32)],
        compiler_params=pltpu.CompilerParams(vmem_limit_bytes=SMALL),
        cost_estimate=pl.CostEstimate(flops=900_000_000 * count, bytes_accessed=700_000 * count, transcendentals=0),
        name="schwarz",
    )(wait, field, y1, y2, m1, m2, *tabs)


def early_kernel(
    wait_ref, sep_ref, own_ref, f_ref, pz_hbm, tile_hbm,
    v_ref, keep_ref, last_ref, pz_ref, tile_ref,
    nv_ref, sems,
):
    copies = []
    pairs = [(f_ref.at[:, pl.ds(CUT, LEVELS * SEP - CUT)], keep_ref), (pz_hbm, pz_ref)]
    pairs.append((tile_hbm, tile_ref))
    for k, (src, dst) in enumerate(pairs):
        copies.append(pltpu.make_async_copy(src, dst, sems.at[k]))
        copies[-1].start()
    lane = lax.broadcasted_iota(jnp.int32, (4, 128), 1)
    sep = pltpu.roll(jnp.concatenate([sep_ref[...], jnp.zeros((4, CUT), F32)], axis=0), LEAF, 1)
    first = jnp.where(lane < LEAF, own_ref[...], sep[:4, :128])
    first = jnp.concatenate([first, jnp.zeros((4, 128), F32)], axis=0)
    nv_ref[:, :128] = first.astype(BF)
    nv_ref[:, 128:] = sep[:, 128:].astype(BF)
    last_ref[:, LEAF:] = jnp.zeros((VLOC, 128 - LEAF), BF)
    last_ref[:, :LEAF] = f_ref[:, LEVELS * SEP :]
    v_ref[:, VLOC:] = jnp.zeros((8, 640 - VLOC), F32)
    v_ref[:, :VLOC] = dot(nv_ref[...], f_ref[:, :CUT], NT)
    for copy in copies:
        copy.wait()


def early(wait, sep, own, factor):
    pz = np.zeros((128, 384), np.float32)
    pz[:65] = line_table(prolong_np, 64).T
    tile = np.zeros((640, 128), ml_dtypes.bfloat16)
    for ab in range(9):
        for c in range(65):
            tile[ab * 65 + c, c] = 1
    vm = pl.BlockSpec(memory_space=pltpu.VMEM)
    return pl.pallas_call(
        early_kernel,
        in_specs=[UNUSED, vm, vm, vm, HBM, HBM],
        out_specs=[vm] * 5,
        out_shape=[
            jax.ShapeDtypeStruct((8, 640), F32),
            jax.ShapeDtypeStruct((VLOC, LEVELS * SEP - CUT), BF),
            jax.ShapeDtypeStruct((VLOC, 128), BF),
            jax.ShapeDtypeStruct((2, 128, 384), BF),
            jax.ShapeDtypeStruct((640, 128), BF),
        ],
        scratch_shapes=[
            pltpu.VMEM((8, CUT), BF),
            pltpu.SemaphoreType.DMA((3,)),
        ],
        compiler_params=pltpu.CompilerParams(vmem_limit_bytes=SMALL),
        cost_estimate=pl.CostEstimate(flops=2 * 8 * VLOC * CUT, bytes_accessed=9_000_000, transcendentals=0),
        name="early",
    )(wait, sep, own, factor, jnp.stack([jnp.asarray(v) for v in split_np(pz)]), jnp.asarray(tile))


def late_kernel(top_ref, v_ref, keep_ref, last_ref, s_ref, pz_ref, tile_ref, out_ref):
    nv = jnp.concatenate([top_ref[...], jnp.zeros((4, TAIL_WIDE), F32)], axis=0).astype(BF)
    v = v_ref[...]
    add = dot(nv[:, : LEVELS * SEP - CUT], keep_ref[...], NT)
    add = add + dot(nv[:, LEVELS * SEP - CUT :], last_ref[...], NT)
    v = v + jnp.concatenate([add, jnp.zeros((8, 640 - VLOC), F32)], axis=1)
    spread = jnp.where(ab_mask(72, 640), jnp.concatenate([v] * 9, axis=0), 0.0)
    hi, lo = split(spread)
    vert = dot(hi, tile_ref[...]) + dot(lo, tile_ref[...])
    lines = dot3(split(vert), (pz_ref[0], pz_ref[1]))
    p0 = [float(q) for q in prolong_np[0]]
    p1 = [float(q) for q in prolong_np[1]]
    for y in range(12):
        b, j = divmod(y, 6)
        planes = []
        for a in range(3):
            low = lines[(a * 3 + b) * 8 : (a * 3 + b) * 8 + 4, :]
            high = lines[(a * 3 + b + 1) * 8 : (a * 3 + b + 1) * 8 + 4, :]
            planes.append(p0[j] * low + p1[j] * high)
        for x in range(12):
            e, i = divmod(x, 6)
            out_ref[x, y] = s_ref[x, y] + (p0[i] * planes[e] + p1[i] * planes[e + 1])


def late(top, vertex, keep, last, solved, pz, tile):
    vm = pl.BlockSpec(memory_space=pltpu.VMEM)
    return pl.pallas_call(
        late_kernel,
        in_specs=[vm] * 7,
        out_specs=vm,
        out_shape=jax.ShapeDtypeStruct((12, 12, 4, 384), F32),
        compiler_params=pltpu.CompilerParams(vmem_limit_bytes=SMALL),
        cost_estimate=pl.CostEstimate(flops=2 * 8 * VLOC * TAIL, bytes_accessed=5_000_000, transcendentals=0),
        name="late",
    )(top, vertex, keep, last, solved, pz, tile)


def exchange(value, mask):
    return lax.ppermute(value, ("gx", "gy"), [(i, i ^ mask) for i in range(128)])


def odd_pairs(value, axis):
    count = lax.axis_size(axis)
    return lax.ppermute(value, axis, [(i, (i + 1) % count if i % 2 else (i - 1) % count) for i in range(count)])


MASKS = (1, 3, 4, 12, 16, 32, 96)


def local(residual, sx, sy, depth_vectors, lam_x, lam_y, lam_z, coarse_factor):
    factor = coarse_factor.reshape(VLOC, COLS)
    field = residual.transpose(1, 2, 0, 3)
    msg, own, y2, x1, x2, kept = forward(field, factor)
    got1 = exchange(msg, 1)
    got2 = odd_pairs(y2, "gy")
    tabs = tables(
        own, sx, sy, depth_vectors.transpose(1, 2, 0).reshape(64, 64), lam_x, lam_y, lam_z.transpose(1, 0)
    )
    sep = msg[:, : LEVELS * SEP] + got1[:, : LEVELS * SEP]
    done = [sep[:, :SEP]]
    sep = sep[:, SEP:]
    for mask in MASKS[1:]:
        sep = sep + exchange(sep, mask)
        done.append(sep[:, :SEP])
        sep = sep[:, SEP:]
    m1, m2 = faces(done[FACES_AFTER - 1], x1, x2, got1, got2)
    m1 = exchange(m1, 16)
    m2 = odd_pairs(m2, "gx")
    parts = [
        schwarz(first, count, done[level - 1], field, got1, got2, m1, m2, tabs)
        for first, count, level in SCHWARZ_AFTER
    ]
    vertex, keep, last, pz, tile = early(done[EARLY_AFTER - 1], jnp.concatenate(done[:5], axis=1), own, kept)
    solved = jnp.concatenate(parts, axis=0).reshape(4, 12, 16, 384)[:, :, :12].transpose(1, 2, 0, 3)
    top = jnp.concatenate([done[4][:, SEP - LEAF :], done[5], done[6], jnp.zeros((4, TAIL_WIDE - TAIL), F32)], axis=1)
    out = late(top, vertex, keep, last, solved, pz, tile)
    return out.transpose(2, 0, 1, 3)


FACES_AFTER = 2
SCHWARZ_AFTER = ((0, 1, 3), (1, 1, 3), (2, 1, 4), (3, 1, 5))
EARLY_AFTER = 5


def solution(mesh):
    return jax.shard_map(
        local,
        mesh=mesh,
        in_specs=(
            P(None, "gx", "gy", None),
            P("gx", None, None),
            P("gy", None, None),
            P(),
            P("gx", None),
            P("gy", None),
            P(),
            P("gx", "gy", None, None),
        ),
        out_specs=P(None, "gx", "gy", None),
        check_vma=False,
    )
```

```python
import jax
import jax.numpy as jnp
import numpy as np
import ml_dtypes
from jax import lax
from jax.experimental import pallas as pl
from jax.experimental.pallas import tpu as pltpu
from jax.sharding import PartitionSpec as P

SEP = 1024
LEAF = 65
LEVELS = 7
VLOC = 585
COLS = 7233
WIDE = 8192
BF = jnp.bfloat16
F32 = jnp.float32

gauss_nodes = [
    -0.932469514203152,
    -0.6612093864662645,
    -0.2386191860831969,
    0.2386191860831969,
    0.6612093864662645,
    0.932469514203152,
]
gauss_weights = [
    0.17132449237917033,
    0.3607615730481386,
    0.46791393457269104,
    0.46791393457269104,
    0.3607615730481386,
    0.17132449237917033,
]
prolong_np = np.stack(
    [(1.0 - np.array(gauss_nodes)) / 2.0, (1.0 + np.array(gauss_nodes)) / 2.0]
).astype(np.float32)
restrict_np = (
    np.stack([(1.0 - np.array(gauss_nodes)) / 2.0, (1.0 + np.array(gauss_nodes)) / 2.0])
    * np.array(gauss_weights)[None, :]
).astype(np.float32)


def line_table(table, elems):
    out = np.zeros((elems * 6, elems + 1), np.float32)
    for c in range(elems):
        for k in range(6):
            out[6 * c + k, c] = table[0, k]
            out[6 * c + k, c + 1] = table[1, k]
    return out


def split_np(x):
    hi = x.astype(ml_dtypes.bfloat16)
    lo = (x - hi.astype(np.float32)).astype(ml_dtypes.bfloat16)
    return hi, lo


def split(x):
    hi = x.astype(BF)
    lo = (x - hi.astype(F32)).astype(BF)
    return hi, lo


def dot(a, b, dims=(((1,), (0,)), ((), ()))):
    return lax.dot_general(a, b, dims, preferred_element_type=F32)


NT = (((1,), (1,)), ((), ()))
TN = (((0,), (0,)), ((), ()))


def dot3(a, b, dims=(((1,), (0,)), ((), ()))):
    return dot(a[0], b[0], dims) + (dot(a[0], b[1], dims) + dot(a[1], b[0], dims))


def ab_mask(rows, cols):
    col = lax.broadcasted_iota(jnp.int32, (rows, cols), 1)
    ab = lax.broadcasted_iota(jnp.int32, (rows, cols), 0) // 8
    return jnp.logical_and(col >= ab * 65, col < ab * 65 + 65)


FACE = 12 * 384
SLAB = 14 * 384
PADDED = 7296
BIG = 58 << 20
ROW_CHUNKS = ((512, 73), (0, 256), (256, 128), (384, 128))
SMALL = 24 << 20
MIDDLE = 48 << 20
HBM = pl.BlockSpec(memory_space=pltpu.HBM)
UNUSED = pl.BlockSpec(memory_space=pl.ANY)


def whole(shape):
    return pl.BlockSpec(shape, lambda i: (0,) * len(shape))


def parities():
    return lax.axis_index("gy") % 2 == 1, lax.axis_index("gx") % 2 == 1


def forward_kernel(
    r_hbm, rz_hbm, tile_hbm, f_ref,
    msg_ref, own_ref, y2_ref, x1_ref, x2_ref,
    r_ref, rz_ref, tile_ref, keep_ref, u_ref, acc_ref, small_sems, sems,
):
    small = []
    for k, (src, dst) in enumerate(((r_hbm, r_ref), (rz_hbm, rz_ref), (tile_hbm, tile_ref))):
        small.append(pltpu.make_async_copy(src, dst, small_sems.at[k]))
        small[-1].start()
    copies = []
    for k, (start, size) in enumerate(ROW_CHUNKS):
        rows = pl.ds(start, size)
        copies.append(pltpu.make_async_copy(f_ref.at[rows, :], keep_ref.at[rows, :], sems.at[k]))
    copies[0].start()

    u_ref[...] = jnp.zeros_like(u_ref)
    small[0].wait()
    for copy in copies[1:]:
        copy.start()
    r0 = [float(v) for v in restrict_np[0]]
    r1 = [float(v) for v in restrict_np[1]]
    for y_elem in range(2):
        sums = []
        for j in range(6):
            y = 6 * y_elem + j
            lows = [r_ref[i, y] for i in range(6)]
            highs = [r_ref[6 + i, y] for i in range(6)]
            sums.append(
                [
                    sum(r0[i] * lows[i] for i in range(6)),
                    sum(r1[i] * lows[i] for i in range(6)) + sum(r0[i] * highs[i] for i in range(6)),
                    sum(r1[i] * highs[i] for i in range(6)),
                ]
            )
        for a in range(3):
            for t, table in ((0, r0), (1, r1)):
                row = (a * 3 + y_elem + t) * 8
                u_ref[row : row + 4, :] += sum(table[j] * sums[j][a] for j in range(6))
    small[1].wait()
    vert = lax.dot_general(
        u_ref[...], rz_ref[...], (((1,), (0,)), ((), ())),
        precision=lax.Precision.HIGHEST, preferred_element_type=F32,
    ).astype(BF)
    small[2].wait()
    spread = dot(vert, tile_ref[...])
    spread = jnp.where(ab_mask(72, 640), spread, 0.0)
    v = sum(spread[8 * k : 8 * k + 8] for k in range(9)).astype(BF)[:, :VLOC]

    gy_odd, gx_odd = parities()
    for i in range(12):
        cols = slice(384 * i, 384 * i + 384)
        low, high = r_ref[i, 0], r_ref[i, 11]
        msg_ref[:, LEVELS * SEP + 384 * i : LEVELS * SEP + 384 * i + 384] = jnp.where(gy_odd, low, high)
        y2_ref[:, cols] = jnp.where(gy_odd, high, low)
        low, high = r_ref[0, i], r_ref[11, i]
        x1_ref[:, cols] = jnp.where(gx_odd, low, high)
        x2_ref[:, cols] = jnp.where(gx_odd, high, low)

    acc_ref[:, LEVELS * SEP :] = jnp.zeros((8, 128), F32)
    for k, (start, size) in enumerate(ROW_CHUNKS):
        copies[k].wait()
        rows = slice(start, start + size)
        product = dot(v[:, rows], keep_ref[rows, :])
        acc_ref[:, :COLS] = product if k == 0 else acc_ref[:, :COLS] + product
    own_ref[...] = acc_ref[:4, :128]
    msg_ref[:, : LEVELS * SEP] = pltpu.roll(acc_ref[...], PADDED - LEAF, 1)[:4, : LEVELS * SEP]


def forward(field, factor):
    rz = np.zeros((384, 128), np.float32)
    rz[:, :65] = line_table(restrict_np, 64)
    tile = np.zeros((128, 640), ml_dtypes.bfloat16)
    for ab in range(9):
        for c in range(65):
            tile[c, ab * 65 + c] = 1
    shapes = [(4, LEVELS * SEP + FACE), (4, 128), (4, FACE), (4, FACE), (4, FACE)]
    vm = pl.BlockSpec(memory_space=pltpu.VMEM)
    return pl.pallas_call(
        forward_kernel,
        in_specs=[HBM] * 4,
        out_specs=[vm] * 5,
        out_shape=[jax.ShapeDtypeStruct(v, F32) for v in shapes],
        scratch_shapes=[
            pltpu.VMEM((12, 12, 4, 384), F32),
            pltpu.VMEM((384, 128), F32),
            pltpu.VMEM((128, 640), BF),
            pltpu.VMEM((VLOC, COLS), BF),
            pltpu.VMEM((72, 384), F32),
            pltpu.VMEM((8, PADDED), F32),
            pltpu.SemaphoreType.DMA((3,)),
            pltpu.SemaphoreType.DMA((len(ROW_CHUNKS),)),
        ],
        compiler_params=pltpu.CompilerParams(vmem_limit_bytes=BIG),
        cost_estimate=pl.CostEstimate(flops=2 * 8 * VLOC * COLS, bytes_accessed=9_500_000, transcendentals=0),
        name="forward",
    )(field, jnp.asarray(rz), jnp.asarray(tile), factor)


def join_kernel(msg_ref, y1_ref, y2_ref, level_ref, rest_ref):
    level_ref[...] = msg_ref[:, :SEP] + y1_ref[:, :SEP]
    rest_ref[...] = msg_ref[:, SEP : LEVELS * SEP] + y1_ref[:, SEP : LEVELS * SEP]


def join(msg, y1, y2):
    vm = pl.BlockSpec(memory_space=pltpu.VMEM)
    return pl.pallas_call(
        join_kernel,
        in_specs=[vm, vm, UNUSED],
        out_specs=[vm] * 2,
        out_shape=[
            jax.ShapeDtypeStruct((4, SEP), F32),
            jax.ShapeDtypeStruct((4, (LEVELS - 1) * SEP), F32),
        ],
        compiler_params=pltpu.CompilerParams(vmem_limit_bytes=MIDDLE),
        cost_estimate=pl.CostEstimate(flops=30_000, bytes_accessed=400_000, transcendentals=0),
        name="join",
    )(msg, y1, y2)


def faces_kernel(wait_ref, x1_ref, x2_ref, y1_ref, y2_ref, m1_ref, m2_ref):
    gy_odd, gx_odd = parities()
    m1_ref[:, :FACE] = x1_ref[...]
    m2_ref[:, :FACE] = x2_ref[...]
    tail = LEVELS * SEP
    low_x = slice(0, 384)
    high_x = slice(FACE - 384, FACE)

    def corner(cols):
        one = y1_ref[:, tail + cols.start : tail + cols.stop]
        two = y2_ref[:, cols]
        return jnp.where(gy_odd, one, two), jnp.where(gy_odd, two, one)

    low, high = corner(low_x), corner(high_x)
    for k in range(2):
        cols = slice(FACE + 384 * k, FACE + 384 * k + 384)
        m1_ref[:, cols] = jnp.where(gx_odd, low[k], high[k])
        m2_ref[:, cols] = jnp.where(gx_odd, high[k], low[k])


def faces(wait, x1, x2, y1, y2):
    vm = pl.BlockSpec(memory_space=pltpu.VMEM)
    return pl.pallas_call(
        faces_kernel,
        in_specs=[UNUSED] + [vm] * 4,
        out_specs=[vm] * 2,
        out_shape=[jax.ShapeDtypeStruct((4, SLAB), F32)] * 2,
        compiler_params=pltpu.CompilerParams(vmem_limit_bytes=SMALL),
        cost_estimate=pl.CostEstimate(flops=100_000, bytes_accessed=300_000, transcendentals=0),
        name="faces",
    )(wait, x1, x2, y1, y2)


def tables_kernel(wait_ref, sx_ref, sy_ref, dt_ref, lx_ref, ly_ref, lz_ref, a_ref, b_ref, zf_ref, zb_ref, rs_ref):
    lane = lax.broadcasted_iota(jnp.int32, (8, 256), 1)
    sub = lax.broadcasted_iota(jnp.int32, (8, 256), 0)
    slab = lane // 16
    xpos = jnp.where(slab < 12, slab + 1, jnp.where(slab == 12, 0, jnp.where(slab == 13, 13, 99)))
    yrow = lane % 16
    ypos = jnp.where(yrow < 12, yrow + 1, jnp.where(yrow == 12, 0, jnp.where(yrow == 13, 13, 99)))
    inner = jnp.logical_and(sub >= 1, sub <= 6)

    def exact(a, b, dims):
        return lax.dot_general(a, b, dims, precision=lax.Precision.HIGHEST, preferred_element_type=F32)

    def expand(mat_ref, pos, keep):
        parts = []
        for e in range(2):
            pick = jnp.where(jnp.logical_and(pos == 6 * e + sub, keep), 1.0, 0.0)
            parts.append(exact(mat_ref[e], pick, TN))
        return jnp.concatenate(parts, axis=0)

    everything = sub >= 0
    ax = expand(sx_ref, xpos, everything)
    ay = expand(sy_ref, ypos, everything)
    for i in range(16):
        hi, lo = split(ax[i : i + 1, :] * ay)
        a_ref[0, 16 * i : 16 * i + 16, :] = hi
        a_ref[1, 16 * i : 16 * i + 16, :] = lo
    bx = expand(sx_ref, xpos, inner)
    by = expand(sy_ref, ypos, inner)
    full = jnp.concatenate([bx[i : i + 1, :] * by for i in range(16)], axis=0)
    hi, lo = split(full.T)
    b_ref[0] = hi
    b_ref[1] = lo

    row = lax.broadcasted_iota(jnp.int32, (256, 8), 0)
    col = lax.broadcasted_iota(jnp.int32, (256, 8), 1)

    def column(lam_ref, group):
        total = jnp.zeros((256, 8), F32)
        for e in range(2):
            total += jnp.where(group == 8 * e + col, lam_ref[e : e + 1, :], 0.0)
        return jnp.sum(total, axis=1, keepdims=True)

    lateral = column(lx_ref, row // 16) + column(ly_ref, row % 16)

    for g in range(2):
        pick = jnp.where(
            lax.broadcasted_iota(jnp.int32, (64, 256), 0)
            == lax.broadcasted_iota(jnp.int32, (64, 256), 1) // 8 + 32 * g,
            1.0,
            0.0,
        )
        mine = sub == lane % 8
        spread = exact(dt_ref[...], pick, (((1,), (0,)), ((), ())))
        depth = exact(lz_ref[...], pick, (((1,), (0,)), ((), ())))
        depth = jnp.sum(jnp.where(mine, depth, 0.0), axis=0, keepdims=True)
        rs_ref[:, 256 * g : 256 * g + 256] = 1.0 / (lateral + depth)
        z = lax.broadcasted_iota(jnp.int32, (256, 256), 0) + 128 * g
        c = lax.broadcasted_iota(jnp.int32, (256, 256), 1) // 8 + 32 * g
        w = z + 1 - 6 * c
        table = jnp.zeros((256, 256), F32)
        for k in range(8):
            line = jnp.sum(jnp.where(mine, spread[8 * k : 8 * k + 8], 0.0), axis=0, keepdims=True)
            table = jnp.where(w == k, line, table)
        hi, lo = split(table)
        zf_ref[0, g] = hi
        zf_ref[1, g] = lo
        mid = jnp.logical_and(w >= 1, w <= 6)
        zb_ref[0, g] = jnp.where(mid, hi.astype(F32), 0.0).astype(BF)
        zb_ref[1, g] = jnp.where(mid, lo.astype(F32), 0.0).astype(BF)


def tables(wait, sx, sy, dt, lx, ly, lz):
    vm = pl.BlockSpec(memory_space=pltpu.VMEM)
    return pl.pallas_call(
        tables_kernel,
        in_specs=[UNUSED] + [vm] * 6,
        out_specs=[vm] * 5,
        out_shape=[
            jax.ShapeDtypeStruct((2, 256, 256), BF),
            jax.ShapeDtypeStruct((2, 256, 256), BF),
            jax.ShapeDtypeStruct((2, 2, 256, 256), BF),
            jax.ShapeDtypeStruct((2, 2, 256, 256), BF),
            jax.ShapeDtypeStruct((256, 512), F32),
        ],
        compiler_params=pltpu.CompilerParams(vmem_limit_bytes=SMALL),
        cost_estimate=pl.CostEstimate(flops=1_000_000_000, bytes_accessed=2_000_000, transcendentals=0),
        name="tables",
    )(wait, sx, sy, dt, lx, ly, lz)


def shifted(left, right):
    pair = jnp.concatenate([left, right], axis=1)
    pair = jnp.concatenate([pair, jnp.zeros((4, 2 * SEP), F32)], axis=0)
    return pltpu.roll(pair, LEAF, 1)[:, SEP:]


def chunk_values(chunk, level_refs):
    if chunk:
        return shifted(level_refs[0][...], level_refs[1][...]).astype(BF)
    own, level = level_refs
    lane = lax.broadcasted_iota(jnp.int32, (4, 128), 1)
    rest = pltpu.roll(jnp.concatenate([level[...], jnp.zeros((4, SEP), F32)], axis=0), LEAF, 1)
    head = jnp.where(lane < LEAF, own[...], rest[:4, :128])
    head = jnp.concatenate([head, jnp.zeros((4, 128), F32)], axis=0)
    return jnp.concatenate([head, rest[:, 128:]], axis=1).astype(BF)


def schwarz_kernel(first, chunks, *refs):
    wait_ref, r_ref, y1_ref, y2_ref, m1_ref, m2_ref, a_ref, b_ref, zf_ref, zb_ref, rs_ref = refs[:11]
    refs = refs[11:]
    level_refs = refs[: len(chunks) + 1] if chunks else ()
    refs = refs[len(level_refs) :]
    if chunks:
        f_ref, out_ref, v_ref, x_ref, chunk_ref, sem = refs
        cols = pl.ds(chunks[0] * SEP, len(chunks) * SEP)
        copy = pltpu.make_async_copy(f_ref.at[:, cols], chunk_ref, sem)
        copy.start()
    else:
        out_ref, x_ref = refs
    schwarz_body(first, r_ref, y1_ref, y2_ref, m1_ref, m2_ref, a_ref, b_ref, zf_ref, zb_ref, rs_ref, out_ref, x_ref)
    if chunks:
        copy.wait()
        total = jnp.zeros((8, VLOC), F32)
        for k, chunk in enumerate(chunks):
            values = chunk_values(chunk, level_refs[k : k + 2])
            total = total + dot(values, chunk_ref[:, k * SEP : k * SEP + SEP], NT)
        v_ref[:, :VLOC] = total
        v_ref[:, VLOC:] = jnp.zeros((8, 640 - VLOC), F32)


def schwarz_body(
    first, r_ref, y1_ref, y2_ref, m1_ref, m2_ref, a_ref, b_ref, zf_ref, zb_ref, rs_ref, out_ref, x_ref
):
    gy_odd, gx_odd = parities()
    tail = LEVELS * SEP
    x_ref[...] = jnp.zeros_like(x_ref)
    for k in range(out_ref.shape[0]):
        n = first + k
        for x in range(12):
            x_ref[k, 16 * x : 16 * x + 12, :] = r_ref[x, :, n, :]
            one = y1_ref[n : n + 1, tail + 384 * x : tail + 384 * x + 384]
            two = y2_ref[n : n + 1, 384 * x : 384 * x + 384]
            x_ref[k, 16 * x + 12 : 16 * x + 13, :] = jnp.where(gy_odd, one, two)
            x_ref[k, 16 * x + 13 : 16 * x + 14, :] = jnp.where(gy_odd, two, one)
        for j in range(14):
            one = m1_ref[n : n + 1, 384 * j : 384 * j + 384]
            two = m2_ref[n : n + 1, 384 * j : 384 * j + 384]
            x_ref[k, 192 + j : 193 + j, :] = jnp.where(gx_odd, one, two)
            x_ref[k, 208 + j : 209 + j, :] = jnp.where(gx_odd, two, one)
        a = (a_ref[0][:, :224], a_ref[1][:, :224])
        t1 = split(dot3(a, split(x_ref[k])))
        backs = []
        for g in range(2):
            part = (t1[0][:, 128 * g : 128 * g + 256], t1[1][:, 128 * g : 128 * g + 256])
            t2 = dot3(part, (zf_ref[0, g], zf_ref[1, g]))
            t3 = split(t2 * rs_ref[:, 256 * g : 256 * g + 256])
            backs.append(dot3(t3, (zb_ref[0, g], zb_ref[1, g]), NT))
        t4 = split(
            jnp.concatenate(
                [backs[0][:, :128], backs[0][:, 128:] + backs[1][:, :128], backs[1][:, 128:]], axis=1
            )
        )
        out_ref[k] = dot3((b_ref[0][:192], b_ref[1][:192]), t4)


def schwarz(first, wait, chunks, levels, factor, field, y1, y2, m1, m2, tabs):
    vm = pl.BlockSpec(memory_space=pltpu.VMEM)
    kernel = lambda *refs: schwarz_kernel(first, chunks, *refs)
    extra = (*levels, factor) if chunks else ()
    out = jax.ShapeDtypeStruct((1, 192, 384), F32)
    scratch = [pltpu.VMEM((1, 224, 384), F32)]
    if chunks:
        scratch += [pltpu.VMEM((VLOC, len(chunks) * SEP), BF), pltpu.SemaphoreType.DMA]
    return pl.pallas_call(
        kernel,
        in_specs=[UNUSED] + [vm] * 10 + ([vm] * len(levels) + [HBM] if chunks else []),
        out_specs=[vm, vm] if chunks else vm,
        out_shape=[out, jax.ShapeDtypeStruct((8, 640), F32)] if chunks else out,
        scratch_shapes=scratch,
        compiler_params=pltpu.CompilerParams(vmem_limit_bytes=MIDDLE),
        cost_estimate=pl.CostEstimate(flops=900_000_000, bytes_accessed=700_000, transcendentals=0),
        name="schwarz",
    )(wait, field, y1, y2, m1, m2, *tabs, *extra)


PACK_LAST = SEP
PACK_PZ = PACK_LAST + 128
PACK_TILE = PACK_PZ + 384
PACK_V = PACK_TILE + 128
PACK = PACK_V + 640


def pack_kernel(*refs):
    l5_ref, l6_ref, v0_ref, v1_ref, v2_ref, const_ref, f_ref, pack_ref, chunk_ref, narrow_ref, sems = refs
    pairs = [
        (f_ref.at[:, pl.ds(5 * SEP, SEP)], chunk_ref),
        (f_ref.at[:, pl.ds(LEVELS * SEP, LEAF)], narrow_ref),
        (f_ref.at[:, pl.ds(6 * SEP, SEP)], pack_ref.at[:, pl.ds(0, SEP)]),
        (const_ref, pack_ref.at[:, pl.ds(PACK_PZ, 512)]),
    ]
    copies = []
    for k, (src, dst) in enumerate(pairs):
        copies.append(pltpu.make_async_copy(src, dst, sems.at[k]))
        copies[-1].start()
    values = shifted(l5_ref[...], l6_ref[...]).astype(BF)
    copies[0].wait()
    v = dot(values, chunk_ref[...], NT)
    v = jnp.concatenate([v, jnp.zeros((8, 640 - VLOC), F32)], axis=1)
    v = v + (v0_ref[...] + (v1_ref[...] + v2_ref[...]))
    for k in range(3):
        term = v.astype(BF)
        v = v - term.astype(F32)
        pack_ref[16 * k : 16 * k + 16, PACK_V:] = jnp.concatenate([term, jnp.zeros((8, 640), BF)], axis=0)
    end = jnp.concatenate([l6_ref[:, SEP - 128 :], jnp.zeros((12, 128), F32)], axis=0)
    end = pltpu.roll(end, LEAF, 1)
    pack_ref[48:64, PACK_V : PACK_V + 128] = end.astype(BF)
    copies[1].wait()
    pack_ref[:, PACK_LAST : PACK_LAST + LEAF] = narrow_ref[...]
    pack_ref[:, PACK_LAST + LEAF : PACK_PZ] = jnp.zeros((VLOC, 128 - LEAF), BF)
    copies[2].wait()
    copies[3].wait()


def packed(l5, l6, v0, v1, v2, factor):
    pz = np.zeros((128, 384), np.float32)
    pz[:65] = line_table(prolong_np, 64).T
    hi, lo = split_np(pz)
    const = np.zeros((VLOC, 512), ml_dtypes.bfloat16)
    const[:128, :384] = hi
    const[128:256, :384] = lo
    for ab in range(9):
        for c in range(65):
            const[ab * 65 + c, 384 + c] = 1
    vm = pl.BlockSpec(memory_space=pltpu.VMEM)
    return pl.pallas_call(
        pack_kernel,
        in_specs=[vm] * 5 + [HBM] * 2,
        out_specs=vm,
        out_shape=jax.ShapeDtypeStruct((VLOC, PACK), BF),
        scratch_shapes=[
            pltpu.VMEM((VLOC, SEP), BF),
            pltpu.VMEM((VLOC, LEAF), BF),
            pltpu.SemaphoreType.DMA((4,)),
        ],
        compiler_params=pltpu.CompilerParams(vmem_limit_bytes=MIDDLE),
        cost_estimate=pl.CostEstimate(flops=2 * 8 * VLOC * SEP, bytes_accessed=4_000_000, transcendentals=0),
        name="pack",
    )(l5, l6, v0, v1, v2, jnp.asarray(const), factor)


def late_kernel(mine_ref, got_ref, pack_ref, s_ref, out_ref):
    top = jnp.concatenate([mine_ref[...] + got_ref[...], jnp.zeros((4, SEP), F32)], axis=0)
    top = pltpu.roll(jnp.concatenate([top, jnp.zeros((8, 128), F32)], axis=1), LEAF, 1)
    lane = lax.broadcasted_iota(jnp.int32, (8, 128), 1)
    head = jnp.where(lane < LEAF, pack_ref[48:64, PACK_V : PACK_V + 128][:8].astype(F32), top[:, :128])
    nv = jnp.concatenate([head, top[:, 128:]], axis=1).astype(BF)
    add = dot(nv, pack_ref[:, :PACK_PZ], NT)
    v = jnp.concatenate([add, jnp.zeros((8, 640 - VLOC), F32)], axis=1)
    for k in range(3):
        v = v + pack_ref[32 - 16 * k : 48 - 16 * k, PACK_V:][:8].astype(F32)
    spread = jnp.where(ab_mask(72, 640), jnp.concatenate([v] * 9, axis=0), 0.0)
    hi, lo = split(spread)
    tile = pack_ref[:, PACK_TILE:PACK_V]
    vert = dot(hi[:, :VLOC], tile) + dot(lo[:, :VLOC], tile)
    tables = (pack_ref[:128, PACK_PZ:PACK_TILE], pack_ref[128:256, PACK_PZ:PACK_TILE])
    lines = dot3(split(vert), tables)
    p0 = [float(q) for q in prolong_np[0]]
    p1 = [float(q) for q in prolong_np[1]]
    for y in range(12):
        b, j = divmod(y, 6)
        planes = []
        for a in range(3):
            low = lines[(a * 3 + b) * 8 : (a * 3 + b) * 8 + 4, :]
            high = lines[(a * 3 + b + 1) * 8 : (a * 3 + b + 1) * 8 + 4, :]
            planes.append(p0[j] * low + p1[j] * high)
        for x in range(12):
            e, i = divmod(x, 6)
            out_ref[x, y] = s_ref[x, y] + (p0[i] * planes[e] + p1[i] * planes[e + 1])


def late(mine, got, pack, solved):
    vm = pl.BlockSpec(memory_space=pltpu.VMEM)
    return pl.pallas_call(
        late_kernel,
        in_specs=[vm] * 4,
        out_specs=vm,
        out_shape=jax.ShapeDtypeStruct((12, 12, 4, 384), F32),
        compiler_params=pltpu.CompilerParams(vmem_limit_bytes=SMALL),
        cost_estimate=pl.CostEstimate(flops=2 * 8 * VLOC * SEP, bytes_accessed=5_000_000, transcendentals=0),
        name="late",
    )(mine, got, pack, solved)


def exchange(value, mask):
    return lax.ppermute(value, ("gx", "gy"), [(i, i ^ mask) for i in range(128)])


def odd_pairs(value, axis):
    count = lax.axis_size(axis)
    return lax.ppermute(value, axis, [(i, (i + 1) % count if i % 2 else (i - 1) % count) for i in range(count)])


MASKS = (1, 3, 4, 12, 16, 32, 96)


def local(residual, sx, sy, depth_vectors, lam_x, lam_y, lam_z, coarse_factor):
    factor = coarse_factor.reshape(VLOC, COLS)
    field = residual.transpose(1, 2, 0, 3)
    msg, own, y2, x1, x2 = forward(field, factor)
    got1 = exchange(msg, 1)
    got2 = odd_pairs(y2, "gy")
    level, sep = join(msg, got1, got2)
    done = [own, level]
    for mask in MASKS[1:-1]:
        sep = sep + exchange(sep, mask)
        done.append(sep[:, :SEP])
        sep = sep[:, SEP:]
    got = exchange(sep, MASKS[-1])
    dt = depth_vectors.transpose(1, 2, 0).reshape(64, 64)
    tabs = tables(done[TABLES_AFTER], sx, sy, dt, lam_x, lam_y, lam_z.transpose(1, 0))
    m1, m2 = faces(tabs[4], x1, x2, got1, got2)
    m1 = exchange(m1, 16)
    m2 = odd_pairs(m2, "gx")
    parts = []
    vertex = []
    for n, (level, chunks) in enumerate(WORK):
        levels = done[chunks[0] : chunks[-1] + 2] if chunks else ()
        part = schwarz(n, done[level], chunks, levels, factor, field, got1, got2, m1, m2, tabs)
        if chunks:
            part, more = part
            vertex.append(more)
        parts.append(part)
    pack = packed(done[5], done[6], *vertex, factor)
    solved = jnp.concatenate(parts, axis=0).reshape(4, 12, 16, 384)[:, :, :12].transpose(1, 2, 0, 3)
    out = late(sep, got, pack, solved)
    return out.transpose(2, 0, 1, 3)


TABLES_AFTER = 1
WORK = ((2, (0, 1)), (3, (2,)), (4, ()), (5, (3, 4)))


def solution(mesh):
    return jax.shard_map(
        local,
        mesh=mesh,
        in_specs=(
            P(None, "gx", "gy", None),
            P("gx", None, None),
            P("gy", None, None),
            P(),
            P("gx", None),
            P("gy", None),
            P(),
            P("gx", "gy", None, None),
        ),
        out_specs=P(None, "gx", "gy", None),
        check_vma=False,
    )
```

```python
import jax
import jax.numpy as jnp
import numpy as np
import ml_dtypes
from jax import lax
from jax.experimental import pallas as pl
from jax.experimental.pallas import tpu as pltpu
from jax.sharding import PartitionSpec as P

SEP = 1024
LEAF = 65
LEVELS = 7
VLOC = 585
COLS = 7233
WIDE = 8192
BF = jnp.bfloat16
F32 = jnp.float32

gauss_nodes = [
    -0.932469514203152,
    -0.6612093864662645,
    -0.2386191860831969,
    0.2386191860831969,
    0.6612093864662645,
    0.932469514203152,
]
gauss_weights = [
    0.17132449237917033,
    0.3607615730481386,
    0.46791393457269104,
    0.46791393457269104,
    0.3607615730481386,
    0.17132449237917033,
]
prolong_np = np.stack(
    [(1.0 - np.array(gauss_nodes)) / 2.0, (1.0 + np.array(gauss_nodes)) / 2.0]
).astype(np.float32)
restrict_np = (
    np.stack([(1.0 - np.array(gauss_nodes)) / 2.0, (1.0 + np.array(gauss_nodes)) / 2.0])
    * np.array(gauss_weights)[None, :]
).astype(np.float32)


def line_table(table, elems):
    out = np.zeros((elems * 6, elems + 1), np.float32)
    for c in range(elems):
        for k in range(6):
            out[6 * c + k, c] = table[0, k]
            out[6 * c + k, c + 1] = table[1, k]
    return out


def split_np(x):
    hi = x.astype(ml_dtypes.bfloat16)
    lo = (x - hi.astype(np.float32)).astype(ml_dtypes.bfloat16)
    return hi, lo


def split(x):
    hi = x.astype(BF)
    lo = (x - hi.astype(F32)).astype(BF)
    return hi, lo


def dot(a, b, dims=(((1,), (0,)), ((), ()))):
    return lax.dot_general(a, b, dims, preferred_element_type=F32)


NT = (((1,), (1,)), ((), ()))
TN = (((0,), (0,)), ((), ()))


def dot3(a, b, dims=(((1,), (0,)), ((), ()))):
    return dot(a[0], b[0], dims) + (dot(a[0], b[1], dims) + dot(a[1], b[0], dims))


def ab_mask(rows, cols):
    col = lax.broadcasted_iota(jnp.int32, (rows, cols), 1)
    ab = lax.broadcasted_iota(jnp.int32, (rows, cols), 0) // 8
    return jnp.logical_and(col >= ab * 65, col < ab * 65 + 65)


FACE = 12 * 384
SLAB = 14 * 384
PADDED = 7296
BIG = 55040 << 10
ROW_CHUNKS = ((512, 73), (0, 256), (256, 128), (384, 128))
SMALL = 24 << 20
MIDDLE = 48 << 20
HBM = pl.BlockSpec(memory_space=pltpu.HBM)
UNUSED = pl.BlockSpec(memory_space=pl.ANY)


def whole(shape):
    return pl.BlockSpec(shape, lambda i: (0,) * len(shape))


def parities():
    return lax.axis_index("gy") % 2 == 1, lax.axis_index("gx") % 2 == 1


def forward_kernel(
    r_hbm, rz_hbm, tile_hbm, f_ref,
    msg_ref, own_ref, y2_ref, x1_ref, x2_ref,
    r_ref, rz_ref, tile_ref, keep_ref, u_ref, acc_ref, small_sems, sems,
):
    small = []
    for k, (src, dst) in enumerate(((r_hbm, r_ref), (rz_hbm, rz_ref), (tile_hbm, tile_ref))):
        small.append(pltpu.make_async_copy(src, dst, small_sems.at[k]))
        small[-1].start()
    copies = []
    for k, (start, size) in enumerate(ROW_CHUNKS):
        rows = pl.ds(start, size)
        copies.append(pltpu.make_async_copy(f_ref.at[rows, :], keep_ref.at[rows, :], sems.at[k]))
    copies[0].start()

    u_ref[...] = jnp.zeros_like(u_ref)
    small[0].wait()
    for copy in copies[1:]:
        copy.start()
    r0 = [float(v) for v in restrict_np[0]]
    r1 = [float(v) for v in restrict_np[1]]
    for y_elem in range(2):
        sums = []
        for j in range(6):
            y = 6 * y_elem + j
            lows = [r_ref[i, y] for i in range(6)]
            highs = [r_ref[6 + i, y] for i in range(6)]
            sums.append(
                [
                    sum(r0[i] * lows[i] for i in range(6)),
                    sum(r1[i] * lows[i] for i in range(6)) + sum(r0[i] * highs[i] for i in range(6)),
                    sum(r1[i] * highs[i] for i in range(6)),
                ]
            )
        for a in range(3):
            for t, table in ((0, r0), (1, r1)):
                row = (a * 3 + y_elem + t) * 8
                u_ref[row : row + 4, :] += sum(table[j] * sums[j][a] for j in range(6))
    small[1].wait()
    vert = lax.dot_general(
        u_ref[...], rz_ref[...], (((1,), (0,)), ((), ())),
        precision=lax.Precision.HIGHEST, preferred_element_type=F32,
    ).astype(BF)
    small[2].wait()
    spread = dot(vert, tile_ref[...])
    spread = jnp.where(ab_mask(72, 640), spread, 0.0)
    v = sum(spread[8 * k : 8 * k + 8] for k in range(9)).astype(BF)[:, :VLOC]

    gy_odd, gx_odd = parities()
    for i in range(12):
        cols = slice(384 * i, 384 * i + 384)
        low, high = r_ref[i, 0], r_ref[i, 11]
        msg_ref[:, LEVELS * SEP + 384 * i : LEVELS * SEP + 384 * i + 384] = jnp.where(gy_odd, low, high)
        y2_ref[:, cols] = jnp.where(gy_odd, high, low)
        low, high = r_ref[0, i], r_ref[11, i]
        x1_ref[:, cols] = jnp.where(gx_odd, low, high)
        x2_ref[:, cols] = jnp.where(gx_odd, high, low)

    acc_ref[:, LEVELS * SEP :] = jnp.zeros((8, 128), F32)
    for k, (start, size) in enumerate(ROW_CHUNKS):
        copies[k].wait()
        rows = slice(start, start + size)
        product = dot(v[:, rows], keep_ref[rows, :])
        acc_ref[:, :COLS] = product if k == 0 else acc_ref[:, :COLS] + product
    own_ref[...] = acc_ref[:4, :128]
    msg_ref[:, : LEVELS * SEP] = pltpu.roll(acc_ref[...], PADDED - LEAF, 1)[:4, : LEVELS * SEP]


def forward(field, factor):
    rz = np.zeros((384, 128), np.float32)
    rz[:, :65] = line_table(restrict_np, 64)
    tile = np.zeros((128, 640), ml_dtypes.bfloat16)
    for ab in range(9):
        for c in range(65):
            tile[c, ab * 65 + c] = 1
    shapes = [(4, LEVELS * SEP + FACE), (4, 128), (4, FACE), (4, FACE), (4, FACE)]
    vm = pl.BlockSpec(memory_space=pltpu.VMEM)
    return pl.pallas_call(
        forward_kernel,
        in_specs=[HBM] * 4,
        out_specs=[vm] * 5,
        out_shape=[jax.ShapeDtypeStruct(v, F32) for v in shapes],
        scratch_shapes=[
            pltpu.VMEM((12, 12, 4, 384), F32),
            pltpu.VMEM((384, 128), F32),
            pltpu.VMEM((128, 640), BF),
            pltpu.VMEM((VLOC, COLS), BF),
            pltpu.VMEM((72, 384), F32),
            pltpu.VMEM((8, PADDED), F32),
            pltpu.SemaphoreType.DMA((3,)),
            pltpu.SemaphoreType.DMA((len(ROW_CHUNKS),)),
        ],
        compiler_params=pltpu.CompilerParams(vmem_limit_bytes=BIG),
        cost_estimate=pl.CostEstimate(flops=2 * 8 * VLOC * COLS, bytes_accessed=9_500_000, transcendentals=0),
        name="forward",
    )(field, jnp.asarray(rz), jnp.asarray(tile), factor)


def join_kernel(wait_ref, msg_ref, y1_ref, y2_ref, level_ref, rest_ref):
    level_ref[...] = msg_ref[:, :SEP] + y1_ref[:, :SEP]
    rest_ref[...] = msg_ref[:, SEP : LEVELS * SEP] + y1_ref[:, SEP : LEVELS * SEP]


def join(wait, msg, y1, y2):
    vm = pl.BlockSpec(memory_space=pltpu.VMEM)
    return pl.pallas_call(
        join_kernel,
        in_specs=[UNUSED, vm, vm, UNUSED],
        out_specs=[vm] * 2,
        out_shape=[
            jax.ShapeDtypeStruct((4, SEP), F32),
            jax.ShapeDtypeStruct((4, (LEVELS - 1) * SEP), F32),
        ],
        compiler_params=pltpu.CompilerParams(vmem_limit_bytes=MIDDLE),
        cost_estimate=pl.CostEstimate(flops=30_000, bytes_accessed=400_000, transcendentals=0),
        name="join",
    )(wait, msg, y1, y2)


def faces_kernel(wait_ref, x1_ref, x2_ref, y1_ref, y2_ref, m1_ref, m2_ref):
    gy_odd, gx_odd = parities()
    m1_ref[:, :FACE] = x1_ref[...]
    m2_ref[:, :FACE] = x2_ref[...]
    tail = LEVELS * SEP
    low_x = slice(0, 384)
    high_x = slice(FACE - 384, FACE)

    def corner(cols):
        one = y1_ref[:, tail + cols.start : tail + cols.stop]
        two = y2_ref[:, cols]
        return jnp.where(gy_odd, one, two), jnp.where(gy_odd, two, one)

    low, high = corner(low_x), corner(high_x)
    for k in range(2):
        cols = slice(FACE + 384 * k, FACE + 384 * k + 384)
        m1_ref[:, cols] = jnp.where(gx_odd, low[k], high[k])
        m2_ref[:, cols] = jnp.where(gx_odd, high[k], low[k])


def faces(wait, x1, x2, y1, y2):
    vm = pl.BlockSpec(memory_space=pltpu.VMEM)
    return pl.pallas_call(
        faces_kernel,
        in_specs=[UNUSED] + [vm] * 4,
        out_specs=[vm] * 2,
        out_shape=[jax.ShapeDtypeStruct((4, SLAB), F32)] * 2,
        compiler_params=pltpu.CompilerParams(vmem_limit_bytes=SMALL),
        cost_estimate=pl.CostEstimate(flops=100_000, bytes_accessed=300_000, transcendentals=0),
        name="faces",
    )(wait, x1, x2, y1, y2)


def tables_kernel(
    wait_ref, r_ref, sx_ref, sy_ref, dt_ref, lx_ref, ly_ref, lz_ref, a_ref, b_ref, zf_ref, zb_ref, rs_ref, xs_ref
):
    xs_ref[...] = jnp.zeros_like(xs_ref)
    for n in range(4):
        for x in range(12):
            xs_ref[n, 16 * x : 16 * x + 12, :] = r_ref[x, :, n, :]
    lane = lax.broadcasted_iota(jnp.int32, (8, 256), 1)
    sub = lax.broadcasted_iota(jnp.int32, (8, 256), 0)
    slab = lane // 16
    xpos = jnp.where(slab < 12, slab + 1, jnp.where(slab == 12, 0, jnp.where(slab == 13, 13, 99)))
    yrow = lane % 16
    ypos = jnp.where(yrow < 12, yrow + 1, jnp.where(yrow == 12, 0, jnp.where(yrow == 13, 13, 99)))
    inner = jnp.logical_and(sub >= 1, sub <= 6)

    def exact(a, b, dims):
        return lax.dot_general(a, b, dims, precision=lax.Precision.HIGHEST, preferred_element_type=F32)

    def expand(mat_ref, pos, keep):
        parts = []
        for e in range(2):
            pick = jnp.where(jnp.logical_and(pos == 6 * e + sub, keep), 1.0, 0.0)
            parts.append(exact(mat_ref[e], pick, TN))
        return jnp.concatenate(parts, axis=0)

    everything = sub >= 0
    ax = expand(sx_ref, xpos, everything)
    ay = expand(sy_ref, ypos, everything)
    for i in range(16):
        hi, lo = split(ax[i : i + 1, :] * ay)
        a_ref[0, 16 * i : 16 * i + 16, :] = hi
        a_ref[1, 16 * i : 16 * i + 16, :] = lo
    bx = expand(sx_ref, xpos, inner)
    by = expand(sy_ref, ypos, inner)
    full = jnp.concatenate([bx[i : i + 1, :] * by for i in range(16)], axis=0)
    hi, lo = split(full.T)
    b_ref[0] = hi
    b_ref[1] = lo

    row = lax.broadcasted_iota(jnp.int32, (256, 8), 0)
    col = lax.broadcasted_iota(jnp.int32, (256, 8), 1)

    def column(lam_ref, group):
        total = jnp.zeros((256, 8), F32)
        for e in range(2):
            total += jnp.where(group == 8 * e + col, lam_ref[e : e + 1, :], 0.0)
        return jnp.sum(total, axis=1, keepdims=True)

    lateral = column(lx_ref, row // 16) + column(ly_ref, row % 16)

    for g in range(2):
        pick = jnp.where(
            lax.broadcasted_iota(jnp.int32, (64, 256), 0)
            == lax.broadcasted_iota(jnp.int32, (64, 256), 1) // 8 + 32 * g,
            1.0,
            0.0,
        )
        mine = sub == lane % 8
        spread = exact(dt_ref[...], pick, (((1,), (0,)), ((), ())))
        depth = exact(lz_ref[...], pick, (((1,), (0,)), ((), ())))
        depth = jnp.sum(jnp.where(mine, depth, 0.0), axis=0, keepdims=True)
        rs_ref[:, 256 * g : 256 * g + 256] = 1.0 / (lateral + depth)
        z = lax.broadcasted_iota(jnp.int32, (256, 256), 0) + 128 * g
        c = lax.broadcasted_iota(jnp.int32, (256, 256), 1) // 8 + 32 * g
        w = z + 1 - 6 * c
        table = jnp.zeros((256, 256), F32)
        for k in range(8):
            line = jnp.sum(jnp.where(mine, spread[8 * k : 8 * k + 8], 0.0), axis=0, keepdims=True)
            table = jnp.where(w == k, line, table)
        hi, lo = split(table)
        zf_ref[0, g] = hi
        zf_ref[1, g] = lo
        mid = jnp.logical_and(w >= 1, w <= 6)
        zb_ref[0, g] = jnp.where(mid, hi.astype(F32), 0.0).astype(BF)
        zb_ref[1, g] = jnp.where(mid, lo.astype(F32), 0.0).astype(BF)


def tables(wait, field, sx, sy, dt, lx, ly, lz):
    vm = pl.BlockSpec(memory_space=pltpu.VMEM)
    return pl.pallas_call(
        tables_kernel,
        in_specs=[UNUSED] + [vm] * 7,
        out_specs=[vm] * 6,
        out_shape=[
            jax.ShapeDtypeStruct((2, 256, 256), BF),
            jax.ShapeDtypeStruct((2, 256, 256), BF),
            jax.ShapeDtypeStruct((2, 2, 256, 256), BF),
            jax.ShapeDtypeStruct((2, 2, 256, 256), BF),
            jax.ShapeDtypeStruct((256, 512), F32),
            jax.ShapeDtypeStruct((4, 224, 384), F32),
        ],
        compiler_params=pltpu.CompilerParams(vmem_limit_bytes=SMALL),
        cost_estimate=pl.CostEstimate(flops=1_000_000_000, bytes_accessed=2_000_000, transcendentals=0),
        name="tables",
    )(wait, field, sx, sy, dt, lx, ly, lz)


def shifted(left, right):
    pair = jnp.concatenate([left, right], axis=1)
    pair = jnp.concatenate([pair, jnp.zeros((4, 2 * SEP), F32)], axis=0)
    return pltpu.roll(pair, LEAF, 1)[:, SEP:]


def chunk_values(chunk, level_refs):
    if chunk:
        return shifted(level_refs[0][...], level_refs[1][...]).astype(BF)
    own, level = level_refs
    lane = lax.broadcasted_iota(jnp.int32, (4, 128), 1)
    rest = pltpu.roll(jnp.concatenate([level[...], jnp.zeros((4, SEP), F32)], axis=0), LEAF, 1)
    head = jnp.where(lane < LEAF, own[...], rest[:4, :128])
    head = jnp.concatenate([head, jnp.zeros((4, 128), F32)], axis=0)
    return jnp.concatenate([head, rest[:, 128:]], axis=1).astype(BF)


def schwarz_kernel(first, chunks, *refs):
    wait_ref, r_ref, y1_ref, y2_ref, m1_ref, m2_ref, a_ref, b_ref, zf_ref, zb_ref, rs_ref = refs[:11]
    refs = refs[11:]
    level_refs = refs[: len(chunks) + 1] if chunks else ()
    refs = refs[len(level_refs) :]
    if chunks:
        f_ref, out_ref, v_ref, x_ref, chunk_ref, sem = refs
        cols = pl.ds(chunks[0] * SEP, len(chunks) * SEP)
        copy = pltpu.make_async_copy(f_ref.at[:, cols], chunk_ref, sem)
        copy.start()
    else:
        out_ref, x_ref = refs
    schwarz_body(first, r_ref, y1_ref, y2_ref, m1_ref, m2_ref, a_ref, b_ref, zf_ref, zb_ref, rs_ref, out_ref, x_ref)
    if chunks:
        copy.wait()
        total = jnp.zeros((8, VLOC), F32)
        for k, chunk in enumerate(chunks):
            values = chunk_values(chunk, level_refs[k : k + 2])
            total = total + dot(values, chunk_ref[:, k * SEP : k * SEP + SEP], NT)
        v_ref[:, :VLOC] = total
        v_ref[:, VLOC:] = jnp.zeros((8, 640 - VLOC), F32)


def schwarz_body(
    first, r_ref, y1_ref, y2_ref, m1_ref, m2_ref, a_ref, b_ref, zf_ref, zb_ref, rs_ref, out_ref, x_ref
):
    gy_odd, gx_odd = parities()
    tail = LEVELS * SEP
    for k in range(out_ref.shape[0]):
        n = first + k
        x_ref[k] = r_ref[n]
        for x in range(12):
            one = y1_ref[n : n + 1, tail + 384 * x : tail + 384 * x + 384]
            two = y2_ref[n : n + 1, 384 * x : 384 * x + 384]
            x_ref[k, 16 * x + 12 : 16 * x + 13, :] = jnp.where(gy_odd, one, two)
            x_ref[k, 16 * x + 13 : 16 * x + 14, :] = jnp.where(gy_odd, two, one)
        for j in range(14):
            one = m1_ref[n : n + 1, 384 * j : 384 * j + 384]
            two = m2_ref[n : n + 1, 384 * j : 384 * j + 384]
            x_ref[k, 192 + j : 193 + j, :] = jnp.where(gx_odd, one, two)
            x_ref[k, 208 + j : 209 + j, :] = jnp.where(gx_odd, two, one)
        a = (a_ref[0][:, :224], a_ref[1][:, :224])
        t1 = split(dot3(a, split(x_ref[k])))
        backs = []
        for g in range(2):
            part = (t1[0][:, 128 * g : 128 * g + 256], t1[1][:, 128 * g : 128 * g + 256])
            t2 = dot3(part, (zf_ref[0, g], zf_ref[1, g]))
            t3 = split(t2 * rs_ref[:, 256 * g : 256 * g + 256])
            backs.append(dot3(t3, (zb_ref[0, g], zb_ref[1, g]), NT))
        t4 = split(
            jnp.concatenate(
                [backs[0][:, :128], backs[0][:, 128:] + backs[1][:, :128], backs[1][:, 128:]], axis=1
            )
        )
        out_ref[k] = dot3((b_ref[0][:192], b_ref[1][:192]), t4)


def schwarz(first, wait, chunks, levels, factor, field, y1, y2, m1, m2, tabs):
    vm = pl.BlockSpec(memory_space=pltpu.VMEM)
    kernel = lambda *refs: schwarz_kernel(first, chunks, *refs)
    extra = (*levels, factor) if chunks else ()
    out = jax.ShapeDtypeStruct((1, 192, 384), F32)
    scratch = [pltpu.VMEM((1, 224, 384), F32)]
    if chunks:
        scratch += [pltpu.VMEM((VLOC, len(chunks) * SEP), BF), pltpu.SemaphoreType.DMA]
    return pl.pallas_call(
        kernel,
        in_specs=[UNUSED] + [vm] * 10 + ([vm] * len(levels) + [HBM] if chunks else []),
        out_specs=[vm, vm] if chunks else vm,
        out_shape=[out, jax.ShapeDtypeStruct((8, 640), F32)] if chunks else out,
        scratch_shapes=scratch,
        compiler_params=pltpu.CompilerParams(vmem_limit_bytes=MIDDLE),
        cost_estimate=pl.CostEstimate(flops=900_000_000, bytes_accessed=700_000, transcendentals=0),
        name="schwarz",
    )(wait, field, y1, y2, m1, m2, *tabs, *extra)


PACK_LAST = SEP
PACK_PZ = PACK_LAST + 128
PACK_TILE = PACK_PZ + 384
PACK_V = PACK_TILE + 128
PACK = PACK_V + 640


def pack_kernel(*refs):
    l5_ref, l6_ref, *vertex_refs, const_ref, f_ref, pack_ref, chunk_ref, narrow_ref, sems = refs
    pairs = [
        (f_ref.at[:, pl.ds(5 * SEP, SEP)], chunk_ref),
        (f_ref.at[:, pl.ds(LEVELS * SEP, LEAF)], narrow_ref),
        (f_ref.at[:, pl.ds(6 * SEP, SEP)], pack_ref.at[:, pl.ds(0, SEP)]),
        (const_ref, pack_ref.at[:, pl.ds(PACK_PZ, 512)]),
    ]
    copies = []
    for k, (src, dst) in enumerate(pairs):
        copies.append(pltpu.make_async_copy(src, dst, sems.at[k]))
        copies[-1].start()
    values = shifted(l5_ref[...], l6_ref[...]).astype(BF)
    copies[0].wait()
    v = dot(values, chunk_ref[...], NT)
    v = jnp.concatenate([v, jnp.zeros((8, 640 - VLOC), F32)], axis=1)
    v = v + sum(ref[...] for ref in vertex_refs)
    for k in range(3):
        term = v.astype(BF)
        v = v - term.astype(F32)
        pack_ref[16 * k : 16 * k + 16, PACK_V:] = jnp.concatenate([term, jnp.zeros((8, 640), BF)], axis=0)
    end = jnp.concatenate([l6_ref[:, SEP - 128 :], jnp.zeros((12, 128), F32)], axis=0)
    end = pltpu.roll(end, LEAF, 1)
    pack_ref[48:64, PACK_V : PACK_V + 128] = end.astype(BF)
    copies[1].wait()
    pack_ref[:, PACK_LAST : PACK_LAST + LEAF] = narrow_ref[...]
    pack_ref[:, PACK_LAST + LEAF : PACK_PZ] = jnp.zeros((VLOC, 128 - LEAF), BF)
    copies[2].wait()
    copies[3].wait()


def packed(l5, l6, vertex, factor):
    pz = np.zeros((128, 384), np.float32)
    pz[:65] = line_table(prolong_np, 64).T
    hi, lo = split_np(pz)
    const = np.zeros((VLOC, 512), ml_dtypes.bfloat16)
    const[:128, :384] = hi
    const[128:256, :384] = lo
    for ab in range(9):
        for c in range(65):
            const[ab * 65 + c, 384 + c] = 1
    vm = pl.BlockSpec(memory_space=pltpu.VMEM)
    return pl.pallas_call(
        pack_kernel,
        in_specs=[vm] * (2 + len(vertex)) + [HBM] * 2,
        out_specs=vm,
        out_shape=jax.ShapeDtypeStruct((VLOC, PACK), BF),
        scratch_shapes=[
            pltpu.VMEM((VLOC, SEP), BF),
            pltpu.VMEM((VLOC, LEAF), BF),
            pltpu.SemaphoreType.DMA((4,)),
        ],
        compiler_params=pltpu.CompilerParams(vmem_limit_bytes=MIDDLE),
        cost_estimate=pl.CostEstimate(flops=2 * 8 * VLOC * SEP, bytes_accessed=4_000_000, transcendentals=0),
        name="pack",
    )(l5, l6, *vertex, jnp.asarray(const), factor)


def late_kernel(mine_ref, got_ref, pack_ref, s_ref, out_ref):
    top = jnp.concatenate([mine_ref[...] + got_ref[...], jnp.zeros((4, SEP), F32)], axis=0)
    top = pltpu.roll(jnp.concatenate([top, jnp.zeros((8, 128), F32)], axis=1), LEAF, 1)
    lane = lax.broadcasted_iota(jnp.int32, (8, 128), 1)
    head = jnp.where(lane < LEAF, pack_ref[48:64, PACK_V : PACK_V + 128][:8].astype(F32), top[:, :128])
    nv = jnp.concatenate([head, top[:, 128:]], axis=1).astype(BF)
    add = dot(nv, pack_ref[:, :PACK_PZ], NT)
    v = jnp.concatenate([add, jnp.zeros((8, 640 - VLOC), F32)], axis=1)
    for k in range(3):
        v = v + pack_ref[32 - 16 * k : 48 - 16 * k, PACK_V:][:8].astype(F32)
    spread = jnp.where(ab_mask(72, 640), jnp.concatenate([v] * 9, axis=0), 0.0)
    hi, lo = split(spread)
    tile = pack_ref[:, PACK_TILE:PACK_V]
    vert = dot(hi[:, :VLOC], tile) + dot(lo[:, :VLOC], tile)
    tables = (pack_ref[:128, PACK_PZ:PACK_TILE], pack_ref[128:256, PACK_PZ:PACK_TILE])
    lines = dot3(split(vert), tables)
    p0 = [float(q) for q in prolong_np[0]]
    p1 = [float(q) for q in prolong_np[1]]
    for y in range(12):
        b, j = divmod(y, 6)
        planes = []
        for a in range(3):
            low = lines[(a * 3 + b) * 8 : (a * 3 + b) * 8 + 4, :]
            high = lines[(a * 3 + b + 1) * 8 : (a * 3 + b + 1) * 8 + 4, :]
            planes.append(p0[j] * low + p1[j] * high)
        for x in range(12):
            e, i = divmod(x, 6)
            out_ref[x, y] = s_ref[x, y] + (p0[i] * planes[e] + p1[i] * planes[e + 1])


def late(mine, got, pack, solved):
    vm = pl.BlockSpec(memory_space=pltpu.VMEM)
    return pl.pallas_call(
        late_kernel,
        in_specs=[vm] * 4,
        out_specs=vm,
        out_shape=jax.ShapeDtypeStruct((12, 12, 4, 384), F32),
        compiler_params=pltpu.CompilerParams(vmem_limit_bytes=SMALL),
        cost_estimate=pl.CostEstimate(flops=2 * 8 * VLOC * SEP, bytes_accessed=5_000_000, transcendentals=0),
        name="late",
    )(mine, got, pack, solved)


def exchange(value, mask):
    return lax.ppermute(value, ("gx", "gy"), [(i, i ^ mask) for i in range(128)])


def odd_pairs(value, axis):
    count = lax.axis_size(axis)
    return lax.ppermute(value, axis, [(i, (i + 1) % count if i % 2 else (i - 1) % count) for i in range(count)])


MASKS = (1, 3, 4, 12, 16, 32, 96)


def local(residual, sx, sy, depth_vectors, lam_x, lam_y, lam_z, coarse_factor):
    factor = coarse_factor.reshape(VLOC, COLS)
    field = residual.transpose(1, 2, 0, 3)
    msg, own, y2, x1, x2 = forward(field, factor)
    got1 = exchange(msg, 1)
    dt = depth_vectors.transpose(1, 2, 0).reshape(64, 64)
    tabs = tables(own, field, sx, sy, dt, lam_x, lam_y, lam_z.transpose(1, 0))
    got2 = odd_pairs(y2, "gy")
    level, sep = join(tabs[4], msg, got1, got2)
    done = [own, level]
    for mask in MASKS[1:-1]:
        sep = sep + exchange(sep, mask)
        done.append(sep[:, :SEP])
        sep = sep[:, SEP:]
    got = exchange(sep, MASKS[-1])
    m1, m2 = faces(done[FACES_AFTER], x1, x2, got1, got2)
    m1 = exchange(m1, 16)
    m2 = odd_pairs(m2, "gx")
    parts = []
    vertex = []
    for n, (level, chunks) in enumerate(WORK):
        levels = done[chunks[0] : chunks[-1] + 2] if chunks else ()
        part = schwarz(n, done[level], chunks, levels, factor, tabs[5], got1, got2, m1, m2, tabs[:5])
        if chunks:
            part, more = part
            vertex.append(more)
        parts.append(part)
    pack = packed(done[5], done[6], vertex, factor)
    solved = jnp.concatenate(parts, axis=0).reshape(4, 12, 16, 384)[:, :, :12].transpose(1, 2, 0, 3)
    out = late(sep, got, pack, solved)
    return out.transpose(2, 0, 1, 3)


FACES_AFTER = 1
WORK = ((2, (0, 1)), (3, (2,)), (4, ()), (5, (3, 4)))


def solution(mesh):
    return jax.shard_map(
        local,
        mesh=mesh,
        in_specs=(
            P(None, "gx", "gy", None),
            P("gx", None, None),
            P("gy", None, None),
            P(),
            P("gx", None),
            P("gy", None),
            P(),
            P("gx", "gy", None, None),
        ),
        out_specs=P(None, "gx", "gy", None),
        check_vma=False,
    )
```

```python
import jax
import jax.numpy as jnp
import numpy as np
import ml_dtypes
from jax import lax
from jax.experimental import pallas as pl
from jax.experimental.pallas import tpu as pltpu
from jax.sharding import PartitionSpec as P

SEP = 1024
LEAF = 65
LEVELS = 7
VLOC = 585
COLS = 7233
WIDE = 8192
BF = jnp.bfloat16
F32 = jnp.float32

gauss_nodes = [
    -0.932469514203152,
    -0.6612093864662645,
    -0.2386191860831969,
    0.2386191860831969,
    0.6612093864662645,
    0.932469514203152,
]
gauss_weights = [
    0.17132449237917033,
    0.3607615730481386,
    0.46791393457269104,
    0.46791393457269104,
    0.3607615730481386,
    0.17132449237917033,
]
prolong_np = np.stack(
    [(1.0 - np.array(gauss_nodes)) / 2.0, (1.0 + np.array(gauss_nodes)) / 2.0]
).astype(np.float32)
restrict_np = (
    np.stack([(1.0 - np.array(gauss_nodes)) / 2.0, (1.0 + np.array(gauss_nodes)) / 2.0])
    * np.array(gauss_weights)[None, :]
).astype(np.float32)


def line_table(table, elems):
    out = np.zeros((elems * 6, elems + 1), np.float32)
    for c in range(elems):
        for k in range(6):
            out[6 * c + k, c] = table[0, k]
            out[6 * c + k, c + 1] = table[1, k]
    return out


def split_np(x):
    hi = x.astype(ml_dtypes.bfloat16)
    lo = (x - hi.astype(np.float32)).astype(ml_dtypes.bfloat16)
    return hi, lo


def split(x):
    hi = x.astype(BF)
    lo = (x - hi.astype(F32)).astype(BF)
    return hi, lo


def dot(a, b, dims=(((1,), (0,)), ((), ()))):
    return lax.dot_general(a, b, dims, preferred_element_type=F32)


NT = (((1,), (1,)), ((), ()))
TN = (((0,), (0,)), ((), ()))


def dot3(a, b, dims=(((1,), (0,)), ((), ()))):
    return dot(a[0], b[0], dims) + (dot(a[0], b[1], dims) + dot(a[1], b[0], dims))


def ab_mask(rows, cols):
    col = lax.broadcasted_iota(jnp.int32, (rows, cols), 1)
    ab = lax.broadcasted_iota(jnp.int32, (rows, cols), 0) // 8
    return jnp.logical_and(col >= ab * 65, col < ab * 65 + 65)


FACE = 12 * 384
SLAB = 14 * 384
PADDED = 7296
BIG = 54272 << 10
ROW_CHUNKS = ((512, 73), (0, 256), (256, 128), (384, 128))
SMALL = 24 << 20
MIDDLE = 48 << 20
HBM = pl.BlockSpec(memory_space=pltpu.HBM)
UNUSED = pl.BlockSpec(memory_space=pl.ANY)


def whole(shape):
    return pl.BlockSpec(shape, lambda i: (0,) * len(shape))


def parities():
    return lax.axis_index("gy") % 2 == 1, lax.axis_index("gx") % 2 == 1


def forward_kernel(
    r_hbm, f_ref,
    msg_ref, own_ref, y2_ref, x1_ref, x2_ref,
    r_ref, keep_ref, u_ref, acc_ref, field_sem, sems,
):
    field_copy = pltpu.make_async_copy(r_hbm, r_ref, field_sem)
    field_copy.start()
    copies = []
    for k, (start, size) in enumerate(ROW_CHUNKS):
        rows = pl.ds(start, size)
        copies.append(pltpu.make_async_copy(f_ref.at[rows, :], keep_ref.at[rows, :], sems.at[k]))
    copies[0].start()

    u_ref[...] = jnp.zeros_like(u_ref)
    z = lax.broadcasted_iota(jnp.int32, (384, 128), 0)
    vertex = lax.broadcasted_iota(jnp.int32, (384, 128), 1)
    elem = z // 6
    low, high = jnp.zeros((384, 128), F32), jnp.zeros((384, 128), F32)
    for k in range(6):
        low = jnp.where(z - 6 * elem == k, float(restrict_np[0, k]), low)
        high = jnp.where(z - 6 * elem == k, float(restrict_np[1, k]), high)
    rz = jnp.where(vertex == elem, low, jnp.where(vertex == elem + 1, high, 0.0))
    place = lax.broadcasted_iota(jnp.int32, (128, 640), 1)
    row = lax.broadcasted_iota(jnp.int32, (128, 640), 0)
    tile = jnp.where(row == place - 65 * (place // 65), 1.0, 0.0).astype(BF)

    field_copy.wait()
    for copy in copies[1:]:
        copy.start()
    r0 = [float(v) for v in restrict_np[0]]
    r1 = [float(v) for v in restrict_np[1]]
    for y_elem in range(2):
        sums = []
        for j in range(6):
            y = 6 * y_elem + j
            lows = [r_ref[i, y] for i in range(6)]
            highs = [r_ref[6 + i, y] for i in range(6)]
            sums.append(
                [
                    sum(r0[i] * lows[i] for i in range(6)),
                    sum(r1[i] * lows[i] for i in range(6)) + sum(r0[i] * highs[i] for i in range(6)),
                    sum(r1[i] * highs[i] for i in range(6)),
                ]
            )
        for a in range(3):
            for t, table in ((0, r0), (1, r1)):
                row = (a * 3 + y_elem + t) * 8
                u_ref[row : row + 4, :] += sum(table[j] * sums[j][a] for j in range(6))
    vert = lax.dot_general(
        u_ref[...], rz, (((1,), (0,)), ((), ())),
        precision=lax.Precision.HIGHEST, preferred_element_type=F32,
    ).astype(BF)
    spread = dot(vert, tile)
    spread = jnp.where(ab_mask(72, 640), spread, 0.0)
    v = sum(spread[8 * k : 8 * k + 8] for k in range(9)).astype(BF)[:, :VLOC]

    gy_odd, gx_odd = parities()
    for i in range(12):
        cols = slice(384 * i, 384 * i + 384)
        low, high = r_ref[i, 0], r_ref[i, 11]
        msg_ref[:, LEVELS * SEP + 384 * i : LEVELS * SEP + 384 * i + 384] = jnp.where(gy_odd, low, high)
        y2_ref[:, cols] = jnp.where(gy_odd, high, low)
        low, high = r_ref[0, i], r_ref[11, i]
        x1_ref[:, cols] = jnp.where(gx_odd, low, high)
        x2_ref[:, cols] = jnp.where(gx_odd, high, low)

    acc_ref[:, LEVELS * SEP :] = jnp.zeros((8, 128), F32)
    for k, (start, size) in enumerate(ROW_CHUNKS):
        copies[k].wait()
        rows = slice(start, start + size)
        product = dot(v[:, rows], keep_ref[rows, :])
        acc_ref[:, :COLS] = product if k == 0 else acc_ref[:, :COLS] + product
    own_ref[...] = acc_ref[:4, :128]
    msg_ref[:, : LEVELS * SEP] = pltpu.roll(acc_ref[...], PADDED - LEAF, 1)[:4, : LEVELS * SEP]


def forward(field, factor):
    shapes = [(4, LEVELS * SEP + FACE), (4, 128), (4, FACE), (4, FACE), (4, FACE)]
    vm = pl.BlockSpec(memory_space=pltpu.VMEM)
    return pl.pallas_call(
        forward_kernel,
        in_specs=[HBM] * 2,
        out_specs=[vm] * 5,
        out_shape=[jax.ShapeDtypeStruct(v, F32) for v in shapes],
        scratch_shapes=[
            pltpu.VMEM((12, 12, 4, 384), F32),
            pltpu.VMEM((VLOC, COLS), BF),
            pltpu.VMEM((72, 384), F32),
            pltpu.VMEM((8, PADDED), F32),
            pltpu.SemaphoreType.DMA,
            pltpu.SemaphoreType.DMA((len(ROW_CHUNKS),)),
        ],
        compiler_params=pltpu.CompilerParams(vmem_limit_bytes=BIG),
        cost_estimate=pl.CostEstimate(flops=2 * 8 * VLOC * COLS, bytes_accessed=9_500_000, transcendentals=0),
        name="forward",
    )(field, factor)


def join_kernel(wait_ref, msg_ref, y1_ref, y2_ref, level_ref, rest_ref):
    level_ref[...] = msg_ref[:, :SEP] + y1_ref[:, :SEP]
    rest_ref[...] = msg_ref[:, SEP : LEVELS * SEP] + y1_ref[:, SEP : LEVELS * SEP]


def join(wait, msg, y1, y2):
    vm = pl.BlockSpec(memory_space=pltpu.VMEM)
    return pl.pallas_call(
        join_kernel,
        in_specs=[UNUSED, vm, vm, UNUSED],
        out_specs=[vm] * 2,
        out_shape=[
            jax.ShapeDtypeStruct((4, SEP), F32),
            jax.ShapeDtypeStruct((4, (LEVELS - 1) * SEP), F32),
        ],
        compiler_params=pltpu.CompilerParams(vmem_limit_bytes=MIDDLE),
        cost_estimate=pl.CostEstimate(flops=30_000, bytes_accessed=400_000, transcendentals=0),
        name="join",
    )(wait, msg, y1, y2)


def faces_kernel(wait_ref, x1_ref, x2_ref, y1_ref, y2_ref, m1_ref, m2_ref):
    gy_odd, gx_odd = parities()
    m1_ref[:, :FACE] = x1_ref[...]
    m2_ref[:, :FACE] = x2_ref[...]
    tail = LEVELS * SEP
    low_x = slice(0, 384)
    high_x = slice(FACE - 384, FACE)

    def corner(cols):
        one = y1_ref[:, tail + cols.start : tail + cols.stop]
        two = y2_ref[:, cols]
        return jnp.where(gy_odd, one, two), jnp.where(gy_odd, two, one)

    low, high = corner(low_x), corner(high_x)
    for k in range(2):
        cols = slice(FACE + 384 * k, FACE + 384 * k + 384)
        m1_ref[:, cols] = jnp.where(gx_odd, low[k], high[k])
        m2_ref[:, cols] = jnp.where(gx_odd, high[k], low[k])


def faces(wait, x1, x2, y1, y2):
    vm = pl.BlockSpec(memory_space=pltpu.VMEM)
    return pl.pallas_call(
        faces_kernel,
        in_specs=[UNUSED] + [vm] * 4,
        out_specs=[vm] * 2,
        out_shape=[jax.ShapeDtypeStruct((4, SLAB), F32)] * 2,
        compiler_params=pltpu.CompilerParams(vmem_limit_bytes=SMALL),
        cost_estimate=pl.CostEstimate(flops=100_000, bytes_accessed=300_000, transcendentals=0),
        name="faces",
    )(wait, x1, x2, y1, y2)


def tables_kernel(
    wait_ref, r_ref, sx_ref, sy_ref, dt_ref, lx_ref, ly_ref, lz_ref, a_ref, b_ref, zf_ref, zb_ref, rs_ref, xs_ref
):
    xs_ref[...] = jnp.zeros_like(xs_ref)
    for n in range(4):
        for x in range(12):
            xs_ref[n, 16 * x : 16 * x + 12, :] = r_ref[x, :, n, :]
    lane = lax.broadcasted_iota(jnp.int32, (8, 256), 1)
    sub = lax.broadcasted_iota(jnp.int32, (8, 256), 0)
    slab = lane // 16
    xpos = jnp.where(slab < 12, slab + 1, jnp.where(slab == 12, 0, jnp.where(slab == 13, 13, 99)))
    yrow = lane % 16
    ypos = jnp.where(yrow < 12, yrow + 1, jnp.where(yrow == 12, 0, jnp.where(yrow == 13, 13, 99)))
    inner = jnp.logical_and(sub >= 1, sub <= 6)

    def exact(a, b, dims):
        return lax.dot_general(a, b, dims, precision=lax.Precision.HIGHEST, preferred_element_type=F32)

    def expand(mat_ref, pos, keep):
        parts = []
        for e in range(2):
            pick = jnp.where(jnp.logical_and(pos == 6 * e + sub, keep), 1.0, 0.0)
            parts.append(exact(mat_ref[e], pick, TN))
        return jnp.concatenate(parts, axis=0)

    everything = sub >= 0
    ax = expand(sx_ref, xpos, everything)
    ay = expand(sy_ref, ypos, everything)
    for i in range(16):
        hi, lo = split(ax[i : i + 1, :] * ay)
        a_ref[0, 16 * i : 16 * i + 16, :] = hi
        a_ref[1, 16 * i : 16 * i + 16, :] = lo
    bx = expand(sx_ref, xpos, inner)
    by = expand(sy_ref, ypos, inner)
    full = jnp.concatenate([bx[i : i + 1, :] * by for i in range(16)], axis=0)
    hi, lo = split(full.T)
    b_ref[0] = hi
    b_ref[1] = lo

    row = lax.broadcasted_iota(jnp.int32, (256, 8), 0)
    col = lax.broadcasted_iota(jnp.int32, (256, 8), 1)

    def column(lam_ref, group):
        total = jnp.zeros((256, 8), F32)
        for e in range(2):
            total += jnp.where(group == 8 * e + col, lam_ref[e : e + 1, :], 0.0)
        return jnp.sum(total, axis=1, keepdims=True)

    lateral = column(lx_ref, row // 16) + column(ly_ref, row % 16)

    for g in range(2):
        pick = jnp.where(
            lax.broadcasted_iota(jnp.int32, (64, 256), 0)
            == lax.broadcasted_iota(jnp.int32, (64, 256), 1) // 8 + 32 * g,
            1.0,
            0.0,
        )
        mine = sub == lane % 8
        spread = exact(dt_ref[...], pick, (((1,), (0,)), ((), ())))
        depth = exact(lz_ref[...], pick, (((1,), (0,)), ((), ())))
        depth = jnp.sum(jnp.where(mine, depth, 0.0), axis=0, keepdims=True)
        rs_ref[:, 256 * g : 256 * g + 256] = 1.0 / (lateral + depth)
        z = lax.broadcasted_iota(jnp.int32, (256, 256), 0) + 128 * g
        c = lax.broadcasted_iota(jnp.int32, (256, 256), 1) // 8 + 32 * g
        w = z + 1 - 6 * c
        table = jnp.zeros((256, 256), F32)
        for k in range(8):
            line = jnp.sum(jnp.where(mine, spread[8 * k : 8 * k + 8], 0.0), axis=0, keepdims=True)
            table = jnp.where(w == k, line, table)
        hi, lo = split(table)
        zf_ref[0, g] = hi
        zf_ref[1, g] = lo
        mid = jnp.logical_and(w >= 1, w <= 6)
        zb_ref[0, g] = jnp.where(mid, hi.astype(F32), 0.0).astype(BF)
        zb_ref[1, g] = jnp.where(mid, lo.astype(F32), 0.0).astype(BF)


def tables(wait, field, sx, sy, dt, lx, ly, lz):
    vm = pl.BlockSpec(memory_space=pltpu.VMEM)
    return pl.pallas_call(
        tables_kernel,
        in_specs=[UNUSED] + [vm] * 7,
        out_specs=[vm] * 6,
        out_shape=[
            jax.ShapeDtypeStruct((2, 256, 256), BF),
            jax.ShapeDtypeStruct((2, 256, 256), BF),
            jax.ShapeDtypeStruct((2, 2, 256, 256), BF),
            jax.ShapeDtypeStruct((2, 2, 256, 256), BF),
            jax.ShapeDtypeStruct((256, 512), F32),
            jax.ShapeDtypeStruct((4, 224, 384), F32),
        ],
        compiler_params=pltpu.CompilerParams(vmem_limit_bytes=SMALL),
        cost_estimate=pl.CostEstimate(flops=1_000_000_000, bytes_accessed=2_000_000, transcendentals=0),
        name="tables",
    )(wait, field, sx, sy, dt, lx, ly, lz)


def shifted(left, right):
    pair = jnp.concatenate([left, right], axis=1)
    pair = jnp.concatenate([pair, jnp.zeros((4, 2 * SEP), F32)], axis=0)
    return pltpu.roll(pair, LEAF, 1)[:, SEP:]


def chunk_values(chunk, level_refs):
    if chunk:
        return shifted(level_refs[0][...], level_refs[1][...]).astype(BF)
    own, level = level_refs
    lane = lax.broadcasted_iota(jnp.int32, (4, 128), 1)
    rest = pltpu.roll(jnp.concatenate([level[...], jnp.zeros((4, SEP), F32)], axis=0), LEAF, 1)
    head = jnp.where(lane < LEAF, own[...], rest[:4, :128])
    head = jnp.concatenate([head, jnp.zeros((4, 128), F32)], axis=0)
    return jnp.concatenate([head, rest[:, 128:]], axis=1).astype(BF)


def schwarz_kernel(first, chunks, *refs):
    wait_ref, r_ref, y1_ref, y2_ref, m1_ref, m2_ref, a_ref, b_ref, zf_ref, zb_ref, rs_ref = refs[:11]
    refs = refs[11:]
    level_refs = refs[: len(chunks) + 1] if chunks else ()
    refs = refs[len(level_refs) :]
    if chunks:
        f_ref, out_ref, v_ref, x_ref, chunk_ref, sem = refs
        cols = pl.ds(chunks[0] * SEP, len(chunks) * SEP)
        copy = pltpu.make_async_copy(f_ref.at[:, cols], chunk_ref, sem)
        copy.start()
    else:
        out_ref, x_ref = refs
    schwarz_body(first, r_ref, y1_ref, y2_ref, m1_ref, m2_ref, a_ref, b_ref, zf_ref, zb_ref, rs_ref, out_ref, x_ref)
    if chunks:
        copy.wait()
        total = jnp.zeros((8, VLOC), F32)
        for k, chunk in enumerate(chunks):
            values = chunk_values(chunk, level_refs[k : k + 2])
            total = total + dot(values, chunk_ref[:, k * SEP : k * SEP + SEP], NT)
        v_ref[:, :VLOC] = total
        v_ref[:, VLOC:] = jnp.zeros((8, 640 - VLOC), F32)


def schwarz_body(
    first, r_ref, y1_ref, y2_ref, m1_ref, m2_ref, a_ref, b_ref, zf_ref, zb_ref, rs_ref, out_ref, x_ref
):
    gy_odd, gx_odd = parities()
    tail = LEVELS * SEP
    for k in range(out_ref.shape[0]):
        n = first + k
        x_ref[k] = r_ref[n]
        for x in range(12):
            one = y1_ref[n : n + 1, tail + 384 * x : tail + 384 * x + 384]
            two = y2_ref[n : n + 1, 384 * x : 384 * x + 384]
            x_ref[k, 16 * x + 12 : 16 * x + 13, :] = jnp.where(gy_odd, one, two)
            x_ref[k, 16 * x + 13 : 16 * x + 14, :] = jnp.where(gy_odd, two, one)
        for j in range(14):
            one = m1_ref[n : n + 1, 384 * j : 384 * j + 384]
            two = m2_ref[n : n + 1, 384 * j : 384 * j + 384]
            x_ref[k, 192 + j : 193 + j, :] = jnp.where(gx_odd, one, two)
            x_ref[k, 208 + j : 209 + j, :] = jnp.where(gx_odd, two, one)
        a = (a_ref[0][:, :224], a_ref[1][:, :224])
        t1 = split(dot3(a, split(x_ref[k])))
        backs = []
        for g in range(2):
            part = (t1[0][:, 128 * g : 128 * g + 256], t1[1][:, 128 * g : 128 * g + 256])
            t2 = dot3(part, (zf_ref[0, g], zf_ref[1, g]))
            t3 = split(t2 * rs_ref[:, 256 * g : 256 * g + 256])
            backs.append(dot3(t3, (zb_ref[0, g], zb_ref[1, g]), NT))
        t4 = split(
            jnp.concatenate(
                [backs[0][:, :128], backs[0][:, 128:] + backs[1][:, :128], backs[1][:, 128:]], axis=1
            )
        )
        out_ref[k] = dot3((b_ref[0][:192], b_ref[1][:192]), t4)


def schwarz(first, wait, chunks, levels, factor, field, y1, y2, m1, m2, tabs):
    vm = pl.BlockSpec(memory_space=pltpu.VMEM)
    kernel = lambda *refs: schwarz_kernel(first, chunks, *refs)
    extra = (*levels, factor) if chunks else ()
    out = jax.ShapeDtypeStruct((1, 192, 384), F32)
    scratch = [pltpu.VMEM((1, 224, 384), F32)]
    if chunks:
        scratch += [pltpu.VMEM((VLOC, len(chunks) * SEP), BF), pltpu.SemaphoreType.DMA]
    return pl.pallas_call(
        kernel,
        in_specs=[UNUSED] + [vm] * 10 + ([vm] * len(levels) + [HBM] if chunks else []),
        out_specs=[vm, vm] if chunks else vm,
        out_shape=[out, jax.ShapeDtypeStruct((8, 640), F32)] if chunks else out,
        scratch_shapes=scratch,
        compiler_params=pltpu.CompilerParams(vmem_limit_bytes=MIDDLE),
        cost_estimate=pl.CostEstimate(flops=900_000_000, bytes_accessed=700_000, transcendentals=0),
        name="schwarz",
    )(wait, field, y1, y2, m1, m2, *tabs, *extra)


PACK_LAST = SEP
PACK_PZ = PACK_LAST + 128
PACK_TILE = PACK_PZ + 384
PACK_V = PACK_TILE + 128
PACK = PACK_V + 640


def pack_kernel(*refs):
    l5_ref, l6_ref, *vertex_refs, const_ref, f_ref, pack_ref, chunk_ref, narrow_ref, sems = refs
    pairs = [
        (f_ref.at[:, pl.ds(5 * SEP, SEP)], chunk_ref),
        (f_ref.at[:, pl.ds(LEVELS * SEP, LEAF)], narrow_ref),
        (f_ref.at[:, pl.ds(6 * SEP, SEP)], pack_ref.at[:, pl.ds(0, SEP)]),
        (const_ref, pack_ref.at[:, pl.ds(PACK_PZ, 512)]),
    ]
    copies = []
    for k, (src, dst) in enumerate(pairs):
        copies.append(pltpu.make_async_copy(src, dst, sems.at[k]))
        copies[-1].start()
    values = shifted(l5_ref[...], l6_ref[...]).astype(BF)
    copies[0].wait()
    v = dot(values, chunk_ref[...], NT)
    v = jnp.concatenate([v, jnp.zeros((8, 640 - VLOC), F32)], axis=1)
    v = v + sum(ref[...] for ref in vertex_refs)
    for k in range(3):
        term = v.astype(BF)
        v = v - term.astype(F32)
        pack_ref[16 * k : 16 * k + 16, PACK_V:] = jnp.concatenate([term, jnp.zeros((8, 640), BF)], axis=0)
    end = jnp.concatenate([l6_ref[:, SEP - 128 :], jnp.zeros((12, 128), F32)], axis=0)
    end = pltpu.roll(end, LEAF, 1)
    pack_ref[48:64, PACK_V : PACK_V + 128] = end.astype(BF)
    copies[1].wait()
    pack_ref[:, PACK_LAST : PACK_LAST + LEAF] = narrow_ref[...]
    pack_ref[:, PACK_LAST + LEAF : PACK_PZ] = jnp.zeros((VLOC, 128 - LEAF), BF)
    copies[2].wait()
    copies[3].wait()


def packed(l5, l6, vertex, factor):
    pz = np.zeros((128, 384), np.float32)
    pz[:65] = line_table(prolong_np, 64).T
    hi, lo = split_np(pz)
    const = np.zeros((VLOC, 512), ml_dtypes.bfloat16)
    const[:128, :384] = hi
    const[128:256, :384] = lo
    for ab in range(9):
        for c in range(65):
            const[ab * 65 + c, 384 + c] = 1
    vm = pl.BlockSpec(memory_space=pltpu.VMEM)
    return pl.pallas_call(
        pack_kernel,
        in_specs=[vm] * (2 + len(vertex)) + [HBM] * 2,
        out_specs=vm,
        out_shape=jax.ShapeDtypeStruct((VLOC, PACK), BF),
        scratch_shapes=[
            pltpu.VMEM((VLOC, SEP), BF),
            pltpu.VMEM((VLOC, LEAF), BF),
            pltpu.SemaphoreType.DMA((4,)),
        ],
        compiler_params=pltpu.CompilerParams(vmem_limit_bytes=MIDDLE),
        cost_estimate=pl.CostEstimate(flops=2 * 8 * VLOC * SEP, bytes_accessed=4_000_000, transcendentals=0),
        name="pack",
    )(l5, l6, *vertex, jnp.asarray(const), factor)


def late_kernel(mine_ref, got_ref, pack_ref, s_ref, out_ref):
    top = jnp.concatenate([mine_ref[...] + got_ref[...], jnp.zeros((4, SEP), F32)], axis=0)
    top = pltpu.roll(jnp.concatenate([top, jnp.zeros((8, 128), F32)], axis=1), LEAF, 1)
    lane = lax.broadcasted_iota(jnp.int32, (8, 128), 1)
    head = jnp.where(lane < LEAF, pack_ref[48:64, PACK_V : PACK_V + 128][:8].astype(F32), top[:, :128])
    nv = jnp.concatenate([head, top[:, 128:]], axis=1).astype(BF)
    add = dot(nv, pack_ref[:, :PACK_PZ], NT)
    v = jnp.concatenate([add, jnp.zeros((8, 640 - VLOC), F32)], axis=1)
    for k in range(3):
        v = v + pack_ref[32 - 16 * k : 48 - 16 * k, PACK_V:][:8].astype(F32)
    spread = jnp.where(ab_mask(72, 640), jnp.concatenate([v] * 9, axis=0), 0.0)
    hi, lo = split(spread)
    tile = pack_ref[:, PACK_TILE:PACK_V]
    vert = dot(hi[:, :VLOC], tile) + dot(lo[:, :VLOC], tile)
    tables = (pack_ref[:128, PACK_PZ:PACK_TILE], pack_ref[128:256, PACK_PZ:PACK_TILE])
    lines = dot3(split(vert), tables)
    p0 = [float(q) for q in prolong_np[0]]
    p1 = [float(q) for q in prolong_np[1]]
    for y in range(12):
        b, j = divmod(y, 6)
        planes = []
        for a in range(3):
            low = lines[(a * 3 + b) * 8 : (a * 3 + b) * 8 + 4, :]
            high = lines[(a * 3 + b + 1) * 8 : (a * 3 + b + 1) * 8 + 4, :]
            planes.append(p0[j] * low + p1[j] * high)
        for x in range(12):
            e, i = divmod(x, 6)
            out_ref[x, y] = s_ref[x, y] + (p0[i] * planes[e] + p1[i] * planes[e + 1])


def late(mine, got, pack, solved):
    vm = pl.BlockSpec(memory_space=pltpu.VMEM)
    return pl.pallas_call(
        late_kernel,
        in_specs=[vm] * 4,
        out_specs=vm,
        out_shape=jax.ShapeDtypeStruct((12, 12, 4, 384), F32),
        compiler_params=pltpu.CompilerParams(vmem_limit_bytes=SMALL),
        cost_estimate=pl.CostEstimate(flops=2 * 8 * VLOC * SEP, bytes_accessed=5_000_000, transcendentals=0),
        name="late",
    )(mine, got, pack, solved)


def exchange(value, mask):
    return lax.ppermute(value, ("gx", "gy"), [(i, i ^ mask) for i in range(128)])


def odd_pairs(value, axis):
    count = lax.axis_size(axis)
    return lax.ppermute(value, axis, [(i, (i + 1) % count if i % 2 else (i - 1) % count) for i in range(count)])


MASKS = (1, 3, 4, 12, 16, 32, 96)


def local(residual, sx, sy, depth_vectors, lam_x, lam_y, lam_z, coarse_factor):
    factor = coarse_factor.reshape(VLOC, COLS)
    field = residual.transpose(1, 2, 0, 3)
    msg, own, y2, x1, x2 = forward(field, factor)
    got1 = exchange(msg, 1)
    dt = depth_vectors.transpose(1, 2, 0).reshape(64, 64)
    tabs = tables(own, field, sx, sy, dt, lam_x, lam_y, lam_z.transpose(1, 0))
    got2 = odd_pairs(y2, "gy")
    level, sep = join(tabs[4], msg, got1, got2)
    done = [own, level]
    for mask in MASKS[1:-1]:
        sep = sep + exchange(sep, mask)
        done.append(sep[:, :SEP])
        sep = sep[:, SEP:]
    got = exchange(sep, MASKS[-1])
    m1, m2 = faces(done[FACES_AFTER], x1, x2, got1, got2)
    m1 = exchange(m1, 16)
    m2 = odd_pairs(m2, "gx")
    parts = []
    vertex = []
    for n, (level, chunks) in enumerate(WORK):
        levels = done[chunks[0] : chunks[-1] + 2] if chunks else ()
        part = schwarz(n, done[level], chunks, levels, factor, tabs[5], got1, got2, m1, m2, tabs[:5])
        if chunks:
            part, more = part
            vertex.append(more)
        parts.append(part)
    pack = packed(done[5], done[6], vertex, factor)
    solved = jnp.concatenate(parts, axis=0).reshape(4, 12, 16, 384)[:, :, :12].transpose(1, 2, 0, 3)
    out = late(sep, got, pack, solved)
    return out.transpose(2, 0, 1, 3)


FACES_AFTER = 1
WORK = ((2, (0, 1)), (3, (2,)), (4, ()), (5, (3, 4)))


def solution(mesh):
    return jax.shard_map(
        local,
        mesh=mesh,
        in_specs=(
            P(None, "gx", "gy", None),
            P("gx", None, None),
            P("gy", None, None),
            P(),
            P("gx", None),
            P("gy", None),
            P(),
            P("gx", "gy", None, None),
        ),
        out_specs=P(None, "gx", "gy", None),
        check_vma=False,
    )
```

```python
import jax
import jax.numpy as jnp
import numpy as np
import ml_dtypes
from jax import lax
from jax.experimental import pallas as pl
from jax.experimental.pallas import tpu as pltpu
from jax.sharding import PartitionSpec as P

SEP = 1024
LEAF = 65
LEVELS = 7
VLOC = 585
COLS = 7233
WIDE = 8192
BF = jnp.bfloat16
F32 = jnp.float32

gauss_nodes = [
    -0.932469514203152,
    -0.6612093864662645,
    -0.2386191860831969,
    0.2386191860831969,
    0.6612093864662645,
    0.932469514203152,
]
gauss_weights = [
    0.17132449237917033,
    0.3607615730481386,
    0.46791393457269104,
    0.46791393457269104,
    0.3607615730481386,
    0.17132449237917033,
]
prolong_np = np.stack(
    [(1.0 - np.array(gauss_nodes)) / 2.0, (1.0 + np.array(gauss_nodes)) / 2.0]
).astype(np.float32)
restrict_np = (
    np.stack([(1.0 - np.array(gauss_nodes)) / 2.0, (1.0 + np.array(gauss_nodes)) / 2.0])
    * np.array(gauss_weights)[None, :]
).astype(np.float32)


def line_table(table, elems):
    out = np.zeros((elems * 6, elems + 1), np.float32)
    for c in range(elems):
        for k in range(6):
            out[6 * c + k, c] = table[0, k]
            out[6 * c + k, c + 1] = table[1, k]
    return out


def split_np(x):
    hi = x.astype(ml_dtypes.bfloat16)
    lo = (x - hi.astype(np.float32)).astype(ml_dtypes.bfloat16)
    return hi, lo


def split(x):
    hi = x.astype(BF)
    lo = (x - hi.astype(F32)).astype(BF)
    return hi, lo


def dot(a, b, dims=(((1,), (0,)), ((), ()))):
    return lax.dot_general(a, b, dims, preferred_element_type=F32)


NT = (((1,), (1,)), ((), ()))
TN = (((0,), (0,)), ((), ()))


def dot3(a, b, dims=(((1,), (0,)), ((), ()))):
    return dot(a[0], b[0], dims) + (dot(a[0], b[1], dims) + dot(a[1], b[0], dims))


def ab_mask(rows, cols):
    col = lax.broadcasted_iota(jnp.int32, (rows, cols), 1)
    ab = lax.broadcasted_iota(jnp.int32, (rows, cols), 0) // 8
    return jnp.logical_and(col >= ab * 65, col < ab * 65 + 65)


FACE = 12 * 384
SLAB = 14 * 384
PADDED = 7296
BIG = 54272 << 10
ROW_CHUNKS = ((512, 73), (0, 256), (256, 128), (384, 128))
SMALL = 24 << 20
MIDDLE = 48 << 20
HBM = pl.BlockSpec(memory_space=pltpu.HBM)
UNUSED = pl.BlockSpec(memory_space=pl.ANY)


def whole(shape):
    return pl.BlockSpec(shape, lambda i: (0,) * len(shape))


def parities():
    return lax.axis_index("gy") % 2 == 1, lax.axis_index("gx") % 2 == 1


def forward_kernel(
    r_hbm, f_ref,
    msg_ref, own_ref, y2_ref, x1_ref, x2_ref,
    r_ref, keep_ref, u_ref, acc_ref, field_sem, sems,
):
    field_copy = pltpu.make_async_copy(r_hbm, r_ref, field_sem)
    field_copy.start()
    copies = []
    for k, (start, size) in enumerate(ROW_CHUNKS):
        rows = pl.ds(start, size)
        copies.append(pltpu.make_async_copy(f_ref.at[rows, :], keep_ref.at[rows, :], sems.at[k]))
    copies[0].start()

    u_ref[...] = jnp.zeros_like(u_ref)
    z = lax.broadcasted_iota(jnp.int32, (384, 128), 0)
    vertex = lax.broadcasted_iota(jnp.int32, (384, 128), 1)
    elem = z // 6
    low, high = jnp.zeros((384, 128), F32), jnp.zeros((384, 128), F32)
    for k in range(6):
        low = jnp.where(z - 6 * elem == k, float(restrict_np[0, k]), low)
        high = jnp.where(z - 6 * elem == k, float(restrict_np[1, k]), high)
    rz = jnp.where(vertex == elem, low, jnp.where(vertex == elem + 1, high, 0.0))
    place = lax.broadcasted_iota(jnp.int32, (128, 640), 1)
    row = lax.broadcasted_iota(jnp.int32, (128, 640), 0)
    tile = jnp.where(row == place - 65 * (place // 65), 1.0, 0.0).astype(BF)

    field_copy.wait()
    for copy in copies[1:]:
        copy.start()
    r0 = [float(v) for v in restrict_np[0]]
    r1 = [float(v) for v in restrict_np[1]]
    for y_elem in range(2):
        sums = []
        for j in range(6):
            y = 6 * y_elem + j
            lows = [r_ref[i, y] for i in range(6)]
            highs = [r_ref[6 + i, y] for i in range(6)]
            sums.append(
                [
                    sum(r0[i] * lows[i] for i in range(6)),
                    sum(r1[i] * lows[i] for i in range(6)) + sum(r0[i] * highs[i] for i in range(6)),
                    sum(r1[i] * highs[i] for i in range(6)),
                ]
            )
        for a in range(3):
            for t, table in ((0, r0), (1, r1)):
                row = (a * 3 + y_elem + t) * 8
                u_ref[row : row + 4, :] += sum(table[j] * sums[j][a] for j in range(6))
    vert = lax.dot_general(
        u_ref[...], rz, (((1,), (0,)), ((), ())),
        precision=lax.Precision.HIGHEST, preferred_element_type=F32,
    ).astype(BF)
    spread = dot(vert, tile)
    spread = jnp.where(ab_mask(72, 640), spread, 0.0)
    v = sum(spread[8 * k : 8 * k + 8] for k in range(9)).astype(BF)[:, :VLOC]

    gy_odd, gx_odd = parities()
    for i in range(12):
        cols = slice(384 * i, 384 * i + 384)
        low, high = r_ref[i, 0], r_ref[i, 11]
        msg_ref[:, LEVELS * SEP + 384 * i : LEVELS * SEP + 384 * i + 384] = jnp.where(gy_odd, low, high)
        y2_ref[:, cols] = jnp.where(gy_odd, high, low)
        low, high = r_ref[0, i], r_ref[11, i]
        x1_ref[:, cols] = jnp.where(gx_odd, low, high)
        x2_ref[:, cols] = jnp.where(gx_odd, high, low)

    acc_ref[:, LEVELS * SEP :] = jnp.zeros((8, 128), F32)
    for k, (start, size) in enumerate(ROW_CHUNKS):
        copies[k].wait()
        rows = slice(start, start + size)
        product = dot(v[:, rows], keep_ref[rows, :])
        acc_ref[:, :COLS] = product if k == 0 else acc_ref[:, :COLS] + product
    own_ref[...] = acc_ref[:4, :128]
    msg_ref[:, : LEVELS * SEP] = pltpu.roll(acc_ref[...], PADDED - LEAF, 1)[:4, : LEVELS * SEP]


def forward(field, factor):
    shapes = [(4, LEVELS * SEP + FACE), (4, 128), (4, FACE), (4, FACE), (4, FACE)]
    vm = pl.BlockSpec(memory_space=pltpu.VMEM)
    return pl.pallas_call(
        forward_kernel,
        in_specs=[HBM] * 2,
        out_specs=[vm] * 5,
        out_shape=[jax.ShapeDtypeStruct(v, F32) for v in shapes],
        scratch_shapes=[
            pltpu.VMEM((12, 12, 4, 384), F32),
            pltpu.VMEM((VLOC, COLS), BF),
            pltpu.VMEM((72, 384), F32),
            pltpu.VMEM((8, PADDED), F32),
            pltpu.SemaphoreType.DMA,
            pltpu.SemaphoreType.DMA((len(ROW_CHUNKS),)),
        ],
        compiler_params=pltpu.CompilerParams(vmem_limit_bytes=BIG),
        cost_estimate=pl.CostEstimate(flops=2 * 8 * VLOC * COLS, bytes_accessed=9_500_000, transcendentals=0),
        name="forward",
    )(field, factor)


def join_kernel(wait_ref, msg_ref, y1_ref, y2_ref, level_ref, rest_ref):
    level_ref[...] = msg_ref[:, :SEP] + y1_ref[:, :SEP]
    rest_ref[...] = msg_ref[:, SEP : LEVELS * SEP] + y1_ref[:, SEP : LEVELS * SEP]


def join(wait, msg, y1, y2):
    vm = pl.BlockSpec(memory_space=pltpu.VMEM)
    return pl.pallas_call(
        join_kernel,
        in_specs=[UNUSED, vm, vm, UNUSED],
        out_specs=[vm] * 2,
        out_shape=[
            jax.ShapeDtypeStruct((4, SEP), F32),
            jax.ShapeDtypeStruct((4, (LEVELS - 1) * SEP), F32),
        ],
        compiler_params=pltpu.CompilerParams(vmem_limit_bytes=MIDDLE),
        cost_estimate=pl.CostEstimate(flops=30_000, bytes_accessed=400_000, transcendentals=0),
        name="join",
    )(wait, msg, y1, y2)


def faces_kernel(wait_ref, x1_ref, x2_ref, y1_ref, y2_ref, m1_ref, m2_ref):
    gy_odd, gx_odd = parities()
    m1_ref[:, :FACE] = x1_ref[...]
    m2_ref[:, :FACE] = x2_ref[...]
    tail = LEVELS * SEP
    low_x = slice(0, 384)
    high_x = slice(FACE - 384, FACE)

    def corner(cols):
        one = y1_ref[:, tail + cols.start : tail + cols.stop]
        two = y2_ref[:, cols]
        return jnp.where(gy_odd, one, two), jnp.where(gy_odd, two, one)

    low, high = corner(low_x), corner(high_x)
    for k in range(2):
        cols = slice(FACE + 384 * k, FACE + 384 * k + 384)
        m1_ref[:, cols] = jnp.where(gx_odd, low[k], high[k])
        m2_ref[:, cols] = jnp.where(gx_odd, high[k], low[k])


def faces(wait, x1, x2, y1, y2):
    vm = pl.BlockSpec(memory_space=pltpu.VMEM)
    return pl.pallas_call(
        faces_kernel,
        in_specs=[UNUSED] + [vm] * 4,
        out_specs=[vm] * 2,
        out_shape=[jax.ShapeDtypeStruct((4, SLAB), F32)] * 2,
        compiler_params=pltpu.CompilerParams(vmem_limit_bytes=SMALL),
        cost_estimate=pl.CostEstimate(flops=100_000, bytes_accessed=300_000, transcendentals=0),
        name="faces",
    )(wait, x1, x2, y1, y2)


def tables_kernel(
    wait_ref, r_ref, sx_ref, sy_ref, dt_ref, lx_ref, ly_ref, lz_ref, a_ref, b_ref, zf_ref, zb_ref, rs_ref, xs_ref
):
    xs_ref[...] = jnp.zeros_like(xs_ref)
    for n in range(4):
        for x in range(12):
            xs_ref[n, 16 * x : 16 * x + 12, :] = r_ref[x, :, n, :]
    lane = lax.broadcasted_iota(jnp.int32, (8, 256), 1)
    sub = lax.broadcasted_iota(jnp.int32, (8, 256), 0)
    slab = lane // 16
    xpos = jnp.where(slab < 12, slab + 1, jnp.where(slab == 12, 0, jnp.where(slab == 13, 13, 99)))
    yrow = lane % 16
    ypos = jnp.where(yrow < 12, yrow + 1, jnp.where(yrow == 12, 0, jnp.where(yrow == 13, 13, 99)))
    inner = jnp.logical_and(sub >= 1, sub <= 6)

    def exact(a, b, dims):
        return lax.dot_general(a, b, dims, precision=lax.Precision.HIGHEST, preferred_element_type=F32)

    def expand(mat_ref, pos, keep):
        parts = []
        for e in range(2):
            pick = jnp.where(jnp.logical_and(pos == 6 * e + sub, keep), 1.0, 0.0)
            parts.append(exact(mat_ref[e], pick, TN))
        return jnp.concatenate(parts, axis=0)

    everything = sub >= 0
    ax = expand(sx_ref, xpos, everything)
    ay = expand(sy_ref, ypos, everything)
    for i in range(16):
        hi, lo = split(ax[i : i + 1, :] * ay)
        a_ref[0, 16 * i : 16 * i + 16, :] = hi
        a_ref[1, 16 * i : 16 * i + 16, :] = lo
    bx = expand(sx_ref, xpos, inner)
    by = expand(sy_ref, ypos, inner)
    full = jnp.concatenate([bx[i : i + 1, :] * by for i in range(16)], axis=0)
    hi, lo = split(full.T)
    b_ref[0] = hi
    b_ref[1] = lo

    row = lax.broadcasted_iota(jnp.int32, (256, 8), 0)
    col = lax.broadcasted_iota(jnp.int32, (256, 8), 1)

    def column(lam_ref, group):
        total = jnp.zeros((256, 8), F32)
        for e in range(2):
            total += jnp.where(group == 8 * e + col, lam_ref[e : e + 1, :], 0.0)
        return jnp.sum(total, axis=1, keepdims=True)

    lateral = column(lx_ref, row // 16) + column(ly_ref, row % 16)

    for g in range(2):
        pick = jnp.where(
            lax.broadcasted_iota(jnp.int32, (64, 256), 0)
            == lax.broadcasted_iota(jnp.int32, (64, 256), 1) // 8 + 32 * g,
            1.0,
            0.0,
        )
        mine = sub == lane % 8
        spread = exact(dt_ref[...], pick, (((1,), (0,)), ((), ())))
        depth = exact(lz_ref[...], pick, (((1,), (0,)), ((), ())))
        depth = jnp.sum(jnp.where(mine, depth, 0.0), axis=0, keepdims=True)
        rs_ref[:, 256 * g : 256 * g + 256] = 1.0 / (lateral + depth)
        z = lax.broadcasted_iota(jnp.int32, (256, 256), 0) + 128 * g
        c = lax.broadcasted_iota(jnp.int32, (256, 256), 1) // 8 + 32 * g
        w = z + 1 - 6 * c
        table = jnp.zeros((256, 256), F32)
        for k in range(8):
            line = jnp.sum(jnp.where(mine, spread[8 * k : 8 * k + 8], 0.0), axis=0, keepdims=True)
            table = jnp.where(w == k, line, table)
        hi, lo = split(table)
        zf_ref[0, g] = hi
        zf_ref[1, g] = lo
        mid = jnp.logical_and(w >= 1, w <= 6)
        zb_ref[0, g] = jnp.where(mid, hi.astype(F32), 0.0).astype(BF)
        zb_ref[1, g] = jnp.where(mid, lo.astype(F32), 0.0).astype(BF)


def tables(wait, field, sx, sy, dt, lx, ly, lz):
    vm = pl.BlockSpec(memory_space=pltpu.VMEM)
    return pl.pallas_call(
        tables_kernel,
        in_specs=[UNUSED] + [vm] * 7,
        out_specs=[vm] * 6,
        out_shape=[
            jax.ShapeDtypeStruct((2, 256, 256), BF),
            jax.ShapeDtypeStruct((2, 256, 256), BF),
            jax.ShapeDtypeStruct((2, 2, 256, 256), BF),
            jax.ShapeDtypeStruct((2, 2, 256, 256), BF),
            jax.ShapeDtypeStruct((256, 512), F32),
            jax.ShapeDtypeStruct((4, 224, 384), F32),
        ],
        compiler_params=pltpu.CompilerParams(vmem_limit_bytes=SMALL),
        cost_estimate=pl.CostEstimate(flops=1_000_000_000, bytes_accessed=2_000_000, transcendentals=0),
        name="tables",
    )(wait, field, sx, sy, dt, lx, ly, lz)


def shifted(left, right):
    pair = jnp.concatenate([left, right], axis=1)
    pair = jnp.concatenate([pair, jnp.zeros((4, 2 * SEP), F32)], axis=0)
    return pltpu.roll(pair, LEAF, 1)[:, SEP:]


def chunk_values(chunk, level_refs):
    if chunk:
        return shifted(level_refs[0][...], level_refs[1][...]).astype(BF)
    own, level = level_refs
    lane = lax.broadcasted_iota(jnp.int32, (4, 128), 1)
    rest = pltpu.roll(jnp.concatenate([level[...], jnp.zeros((4, SEP), F32)], axis=0), LEAF, 1)
    head = jnp.where(lane < LEAF, own[...], rest[:4, :128])
    head = jnp.concatenate([head, jnp.zeros((4, 128), F32)], axis=0)
    return jnp.concatenate([head, rest[:, 128:]], axis=1).astype(BF)


def schwarz_kernel(first, chunks, *refs):
    wait_ref, r_ref, y1_ref, y2_ref, m1_ref, m2_ref, a_ref, b_ref, zf_ref, zb_ref, rs_ref = refs[:11]
    refs = refs[11:]
    level_refs = refs[: len(chunks) + 1] if chunks else ()
    refs = refs[len(level_refs) :]
    if chunks:
        f_ref, out_ref, v_ref, x_ref, chunk_ref, sem = refs
        cols = pl.ds(chunks[0] * SEP, len(chunks) * SEP)
        copy = pltpu.make_async_copy(f_ref.at[:, cols], chunk_ref, sem)
        copy.start()
    else:
        out_ref, x_ref = refs
    schwarz_body(first, r_ref, y1_ref, y2_ref, m1_ref, m2_ref, a_ref, b_ref, zf_ref, zb_ref, rs_ref, out_ref, x_ref)
    if chunks:
        copy.wait()
        total = jnp.zeros((8, VLOC), F32)
        for k, chunk in enumerate(chunks):
            values = chunk_values(chunk, level_refs[k : k + 2])
            total = total + dot(values, chunk_ref[:, k * SEP : k * SEP + SEP], NT)
        v_ref[:, :VLOC] = total
        v_ref[:, VLOC:] = jnp.zeros((8, 640 - VLOC), F32)


def schwarz_body(
    first, r_ref, y1_ref, y2_ref, m1_ref, m2_ref, a_ref, b_ref, zf_ref, zb_ref, rs_ref, out_ref, x_ref
):
    gy_odd, gx_odd = parities()
    tail = LEVELS * SEP
    for k in range(out_ref.shape[0]):
        n = first + k
        x_ref[k] = r_ref[n]
        for x in range(12):
            one = y1_ref[n : n + 1, tail + 384 * x : tail + 384 * x + 384]
            two = y2_ref[n : n + 1, 384 * x : 384 * x + 384]
            x_ref[k, 16 * x + 12 : 16 * x + 13, :] = jnp.where(gy_odd, one, two)
            x_ref[k, 16 * x + 13 : 16 * x + 14, :] = jnp.where(gy_odd, two, one)
        for j in range(14):
            one = m1_ref[n : n + 1, 384 * j : 384 * j + 384]
            two = m2_ref[n : n + 1, 384 * j : 384 * j + 384]
            x_ref[k, 192 + j : 193 + j, :] = jnp.where(gx_odd, one, two)
            x_ref[k, 208 + j : 209 + j, :] = jnp.where(gx_odd, two, one)
        a = (a_ref[0][:, :224], a_ref[1][:, :224])
        t1 = split(dot3(a, split(x_ref[k])))
        backs = []
        for g in range(2):
            part = (t1[0][:, 128 * g : 128 * g + 256], t1[1][:, 128 * g : 128 * g + 256])
            t2 = dot3(part, (zf_ref[0, g], zf_ref[1, g]))
            t3 = split(t2 * rs_ref[:, 256 * g : 256 * g + 256])
            backs.append(dot3(t3, (zb_ref[0, g], zb_ref[1, g]), NT))
        t4 = split(
            jnp.concatenate(
                [backs[0][:, :128], backs[0][:, 128:] + backs[1][:, :128], backs[1][:, 128:]], axis=1
            )
        )
        res = dot3((b_ref[0][:192], b_ref[1][:192]), t4)
        for x in range(12):
            out_ref[k, x] = res[16 * x : 16 * x + 12, :]


def schwarz(first, wait, chunks, levels, factor, field, y1, y2, m1, m2, tabs):
    vm = pl.BlockSpec(memory_space=pltpu.VMEM)
    kernel = lambda *refs: schwarz_kernel(first, chunks, *refs)
    extra = (*levels, factor) if chunks else ()
    out = jax.ShapeDtypeStruct((1, 12, 12, 384), F32)
    scratch = [pltpu.VMEM((1, 224, 384), F32)]
    if chunks:
        scratch += [pltpu.VMEM((VLOC, len(chunks) * SEP), BF), pltpu.SemaphoreType.DMA]
    return pl.pallas_call(
        kernel,
        in_specs=[UNUSED] + [vm] * 10 + ([vm] * len(levels) + [HBM] if chunks else []),
        out_specs=[vm, vm] if chunks else vm,
        out_shape=[out, jax.ShapeDtypeStruct((8, 640), F32)] if chunks else out,
        scratch_shapes=scratch,
        compiler_params=pltpu.CompilerParams(vmem_limit_bytes=MIDDLE),
        cost_estimate=pl.CostEstimate(flops=900_000_000, bytes_accessed=700_000, transcendentals=0),
        name="schwarz",
    )(wait, field, y1, y2, m1, m2, *tabs, *extra)


PACK_LAST = SEP
PACK_PZ = PACK_LAST + 128
PACK_TILE = PACK_PZ + 384
PACK_V = PACK_TILE + 128
PACK = PACK_V + 640


def pack_kernel(*refs):
    l5_ref, l6_ref, *vertex_refs, const_ref, f_ref, pack_ref, chunk_ref, narrow_ref, sems = refs
    pairs = [
        (f_ref.at[:, pl.ds(5 * SEP, SEP)], chunk_ref),
        (f_ref.at[:, pl.ds(LEVELS * SEP, LEAF)], narrow_ref),
        (f_ref.at[:, pl.ds(6 * SEP, SEP)], pack_ref.at[:, pl.ds(0, SEP)]),
        (const_ref, pack_ref.at[:, pl.ds(PACK_PZ, 512)]),
    ]
    copies = []
    for k, (src, dst) in enumerate(pairs):
        copies.append(pltpu.make_async_copy(src, dst, sems.at[k]))
        copies[-1].start()
    values = shifted(l5_ref[...], l6_ref[...]).astype(BF)
    copies[0].wait()
    v = dot(values, chunk_ref[...], NT)
    v = jnp.concatenate([v, jnp.zeros((8, 640 - VLOC), F32)], axis=1)
    v = v + sum(ref[...] for ref in vertex_refs)
    for k in range(3):
        term = v.astype(BF)
        v = v - term.astype(F32)
        pack_ref[16 * k : 16 * k + 16, PACK_V:] = jnp.concatenate([term, jnp.zeros((8, 640), BF)], axis=0)
    end = jnp.concatenate([l6_ref[:, SEP - 128 :], jnp.zeros((12, 128), F32)], axis=0)
    end = pltpu.roll(end, LEAF, 1)
    pack_ref[48:64, PACK_V : PACK_V + 128] = end.astype(BF)
    copies[1].wait()
    pack_ref[:, PACK_LAST : PACK_LAST + LEAF] = narrow_ref[...]
    pack_ref[:, PACK_LAST + LEAF : PACK_PZ] = jnp.zeros((VLOC, 128 - LEAF), BF)
    copies[2].wait()
    copies[3].wait()


def packed(l5, l6, vertex, factor):
    pz = np.zeros((128, 384), np.float32)
    pz[:65] = line_table(prolong_np, 64).T
    hi, lo = split_np(pz)
    const = np.zeros((VLOC, 512), ml_dtypes.bfloat16)
    const[:128, :384] = hi
    const[128:256, :384] = lo
    for ab in range(9):
        for c in range(65):
            const[ab * 65 + c, 384 + c] = 1
    vm = pl.BlockSpec(memory_space=pltpu.VMEM)
    return pl.pallas_call(
        pack_kernel,
        in_specs=[vm] * (2 + len(vertex)) + [HBM] * 2,
        out_specs=vm,
        out_shape=jax.ShapeDtypeStruct((VLOC, PACK), BF),
        scratch_shapes=[
            pltpu.VMEM((VLOC, SEP), BF),
            pltpu.VMEM((VLOC, LEAF), BF),
            pltpu.SemaphoreType.DMA((4,)),
        ],
        compiler_params=pltpu.CompilerParams(vmem_limit_bytes=MIDDLE),
        cost_estimate=pl.CostEstimate(flops=2 * 8 * VLOC * SEP, bytes_accessed=4_000_000, transcendentals=0),
        name="pack",
    )(l5, l6, *vertex, jnp.asarray(const), factor)


def late_kernel(mine_ref, got_ref, pack_ref, s_ref, out_ref):
    top = jnp.concatenate([mine_ref[...] + got_ref[...], jnp.zeros((4, SEP), F32)], axis=0)
    top = pltpu.roll(jnp.concatenate([top, jnp.zeros((8, 128), F32)], axis=1), LEAF, 1)
    lane = lax.broadcasted_iota(jnp.int32, (8, 128), 1)
    head = jnp.where(lane < LEAF, pack_ref[48:64, PACK_V : PACK_V + 128][:8].astype(F32), top[:, :128])
    nv = jnp.concatenate([head, top[:, 128:]], axis=1).astype(BF)
    add = dot(nv, pack_ref[:, :PACK_PZ], NT)
    v = jnp.concatenate([add, jnp.zeros((8, 640 - VLOC), F32)], axis=1)
    for k in range(3):
        v = v + pack_ref[32 - 16 * k : 48 - 16 * k, PACK_V:][:8].astype(F32)
    spread = jnp.where(ab_mask(72, 640), jnp.concatenate([v] * 9, axis=0), 0.0)
    hi, lo = split(spread)
    tile = pack_ref[:, PACK_TILE:PACK_V]
    vert = dot(hi[:, :VLOC], tile) + dot(lo[:, :VLOC], tile)
    tables = (pack_ref[:128, PACK_PZ:PACK_TILE], pack_ref[128:256, PACK_PZ:PACK_TILE])
    lines = dot3(split(vert), tables)
    p0 = [float(q) for q in prolong_np[0]]
    p1 = [float(q) for q in prolong_np[1]]
    for y in range(12):
        b, j = divmod(y, 6)
        planes = []
        for a in range(3):
            low = lines[(a * 3 + b) * 8 : (a * 3 + b) * 8 + 4, :]
            high = lines[(a * 3 + b + 1) * 8 : (a * 3 + b + 1) * 8 + 4, :]
            planes.append(p0[j] * low + p1[j] * high)
        for x in range(12):
            e, i = divmod(x, 6)
            out_ref[x, y] = s_ref[x, y] + (p0[i] * planes[e] + p1[i] * planes[e + 1])


def late(mine, got, pack, solved):
    vm = pl.BlockSpec(memory_space=pltpu.VMEM)
    return pl.pallas_call(
        late_kernel,
        in_specs=[vm] * 4,
        out_specs=vm,
        out_shape=jax.ShapeDtypeStruct((12, 12, 4, 384), F32),
        compiler_params=pltpu.CompilerParams(vmem_limit_bytes=SMALL),
        cost_estimate=pl.CostEstimate(flops=2 * 8 * VLOC * SEP, bytes_accessed=5_000_000, transcendentals=0),
        name="late",
    )(mine, got, pack, solved)


def exchange(value, mask):
    return lax.ppermute(value, ("gx", "gy"), [(i, i ^ mask) for i in range(128)])


def odd_pairs(value, axis):
    count = lax.axis_size(axis)
    return lax.ppermute(value, axis, [(i, (i + 1) % count if i % 2 else (i - 1) % count) for i in range(count)])


MASKS = (1, 3, 4, 12, 16, 32, 96)


def local(residual, sx, sy, depth_vectors, lam_x, lam_y, lam_z, coarse_factor):
    factor = coarse_factor.reshape(VLOC, COLS)
    field = residual.transpose(1, 2, 0, 3)
    msg, own, y2, x1, x2 = forward(field, factor)
    got1 = exchange(msg, 1)
    dt = depth_vectors.transpose(1, 2, 0).reshape(64, 64)
    tabs = tables(own, field, sx, sy, dt, lam_x, lam_y, lam_z.transpose(1, 0))
    got2 = odd_pairs(y2, "gy")
    level, sep = join(tabs[4], msg, got1, got2)
    done = [own, level]
    for mask in MASKS[1:-1]:
        sep = sep + exchange(sep, mask)
        done.append(sep[:, :SEP])
        sep = sep[:, SEP:]
    got = exchange(sep, MASKS[-1])
    m1, m2 = faces(done[FACES_AFTER], x1, x2, got1, got2)
    m1 = exchange(m1, 16)
    m2 = odd_pairs(m2, "gx")
    parts = []
    vertex = []
    for n, (level, chunks) in enumerate(WORK):
        levels = done[chunks[0] : chunks[-1] + 2] if chunks else ()
        part = schwarz(n, done[level], chunks, levels, factor, tabs[5], got1, got2, m1, m2, tabs[:5])
        if chunks:
            part, more = part
            vertex.append(more)
        parts.append(part)
    pack = packed(done[5], done[6], vertex, factor)
    solved = jnp.concatenate(parts, axis=0).transpose(1, 2, 0, 3)
    out = late(sep, got, pack, solved)
    return out.transpose(2, 0, 1, 3)


FACES_AFTER = 1
WORK = ((2, (0, 1)), (3, (2,)), (4, ()), (5, (3, 4)))


def solution(mesh):
    return jax.shard_map(
        local,
        mesh=mesh,
        in_specs=(
            P(None, "gx", "gy", None),
            P("gx", None, None),
            P("gy", None, None),
            P(),
            P("gx", None),
            P("gy", None),
            P(),
            P("gx", "gy", None, None),
        ),
        out_specs=P(None, "gx", "gy", None),
        check_vma=False,
    )
```

```python
import jax
import jax.numpy as jnp
import numpy as np
import ml_dtypes
from jax import lax
from jax.experimental import pallas as pl
from jax.experimental.pallas import tpu as pltpu
from jax.sharding import PartitionSpec as P

SEP = 1024
LEAF = 65
LEVELS = 7
VLOC = 585
COLS = 7233
WIDE = 8192
BF = jnp.bfloat16
F32 = jnp.float32

gauss_nodes = [
    -0.932469514203152,
    -0.6612093864662645,
    -0.2386191860831969,
    0.2386191860831969,
    0.6612093864662645,
    0.932469514203152,
]
gauss_weights = [
    0.17132449237917033,
    0.3607615730481386,
    0.46791393457269104,
    0.46791393457269104,
    0.3607615730481386,
    0.17132449237917033,
]
prolong_np = np.stack(
    [(1.0 - np.array(gauss_nodes)) / 2.0, (1.0 + np.array(gauss_nodes)) / 2.0]
).astype(np.float32)
restrict_np = (
    np.stack([(1.0 - np.array(gauss_nodes)) / 2.0, (1.0 + np.array(gauss_nodes)) / 2.0])
    * np.array(gauss_weights)[None, :]
).astype(np.float32)


def line_table(table, elems):
    out = np.zeros((elems * 6, elems + 1), np.float32)
    for c in range(elems):
        for k in range(6):
            out[6 * c + k, c] = table[0, k]
            out[6 * c + k, c + 1] = table[1, k]
    return out


def split_np(x):
    hi = x.astype(ml_dtypes.bfloat16)
    lo = (x - hi.astype(np.float32)).astype(ml_dtypes.bfloat16)
    return hi, lo


def split(x):
    hi = x.astype(BF)
    lo = (x - hi.astype(F32)).astype(BF)
    return hi, lo


def dot(a, b, dims=(((1,), (0,)), ((), ()))):
    return lax.dot_general(a, b, dims, preferred_element_type=F32)


NT = (((1,), (1,)), ((), ()))
TN = (((0,), (0,)), ((), ()))


def dot3(a, b, dims=(((1,), (0,)), ((), ()))):
    return dot(a[0], b[0], dims) + (dot(a[0], b[1], dims) + dot(a[1], b[0], dims))


def ab_mask(rows, cols):
    col = lax.broadcasted_iota(jnp.int32, (rows, cols), 1)
    ab = lax.broadcasted_iota(jnp.int32, (rows, cols), 0) // 8
    return jnp.logical_and(col >= ab * 65, col < ab * 65 + 65)


FACE = 12 * 384
SLAB = 14 * 384
PADDED = 7296
BIG = 54272 << 10
ROW_CHUNKS = ((512, 73), (0, 256), (256, 128), (384, 128))
SMALL = 24 << 20
MIDDLE = 48 << 20
HBM = pl.BlockSpec(memory_space=pltpu.HBM)
UNUSED = pl.BlockSpec(memory_space=pl.ANY)


def whole(shape):
    return pl.BlockSpec(shape, lambda i: (0,) * len(shape))


def parities():
    return lax.axis_index("gy") % 2 == 1, lax.axis_index("gx") % 2 == 1


def forward_kernel(
    r_hbm, f_ref,
    msg_ref, own_ref, y2_ref, x1_ref, x2_ref,
    r_ref, keep_ref, u_ref, acc_ref, field_sem, sems,
):
    field_copy = pltpu.make_async_copy(r_hbm, r_ref, field_sem)
    field_copy.start()
    copies = []
    for k, (start, size) in enumerate(ROW_CHUNKS):
        rows = pl.ds(start, size)
        copies.append(pltpu.make_async_copy(f_ref.at[rows, :], keep_ref.at[rows, :], sems.at[k]))
    copies[0].start()

    u_ref[...] = jnp.zeros_like(u_ref)
    z = lax.broadcasted_iota(jnp.int32, (384, 128), 0)
    vertex = lax.broadcasted_iota(jnp.int32, (384, 128), 1)
    elem = z // 6
    low, high = jnp.zeros((384, 128), F32), jnp.zeros((384, 128), F32)
    for k in range(6):
        low = jnp.where(z - 6 * elem == k, float(restrict_np[0, k]), low)
        high = jnp.where(z - 6 * elem == k, float(restrict_np[1, k]), high)
    rz = jnp.where(vertex == elem, low, jnp.where(vertex == elem + 1, high, 0.0))
    place = lax.broadcasted_iota(jnp.int32, (128, 640), 1)
    row = lax.broadcasted_iota(jnp.int32, (128, 640), 0)
    tile = jnp.where(row == place - 65 * (place // 65), 1.0, 0.0).astype(BF)

    field_copy.wait()
    for copy in copies[1:]:
        copy.start()
    r0 = [float(v) for v in restrict_np[0]]
    r1 = [float(v) for v in restrict_np[1]]
    for y_elem in range(2):
        sums = []
        for j in range(6):
            y = 6 * y_elem + j
            lows = [r_ref[i, y] for i in range(6)]
            highs = [r_ref[6 + i, y] for i in range(6)]
            sums.append(
                [
                    sum(r0[i] * lows[i] for i in range(6)),
                    sum(r1[i] * lows[i] for i in range(6)) + sum(r0[i] * highs[i] for i in range(6)),
                    sum(r1[i] * highs[i] for i in range(6)),
                ]
            )
        for a in range(3):
            for t, table in ((0, r0), (1, r1)):
                row = (a * 3 + y_elem + t) * 8
                u_ref[row : row + 4, :] += sum(table[j] * sums[j][a] for j in range(6))
    vert = lax.dot_general(
        u_ref[...], rz, (((1,), (0,)), ((), ())),
        precision=lax.Precision.HIGHEST, preferred_element_type=F32,
    ).astype(BF)
    spread = dot(vert, tile)
    spread = jnp.where(ab_mask(72, 640), spread, 0.0)
    v = sum(spread[8 * k : 8 * k + 8] for k in range(9)).astype(BF)[:, :VLOC]

    gy_odd, gx_odd = parities()
    for i in range(12):
        cols = slice(384 * i, 384 * i + 384)
        low, high = r_ref[i, 0], r_ref[i, 11]
        msg_ref[:, LEVELS * SEP + 384 * i : LEVELS * SEP + 384 * i + 384] = jnp.where(gy_odd, low, high)
        y2_ref[:, cols] = jnp.where(gy_odd, high, low)
        low, high = r_ref[0, i], r_ref[11, i]
        x1_ref[:, cols] = jnp.where(gx_odd, low, high)
        x2_ref[:, cols] = jnp.where(gx_odd, high, low)

    acc_ref[:, LEVELS * SEP :] = jnp.zeros((8, 128), F32)
    for k, (start, size) in enumerate(ROW_CHUNKS):
        copies[k].wait()
        rows = slice(start, start + size)
        product = dot(v[:, rows], keep_ref[rows, :])
        acc_ref[:, :COLS] = product if k == 0 else acc_ref[:, :COLS] + product
    own_ref[...] = acc_ref[:4, :128]
    msg_ref[:, : LEVELS * SEP] = pltpu.roll(acc_ref[...], PADDED - LEAF, 1)[:4, : LEVELS * SEP]


def forward(field, factor):
    shapes = [(4, LEVELS * SEP + FACE), (4, 128), (4, FACE), (4, FACE), (4, FACE)]
    vm = pl.BlockSpec(memory_space=pltpu.VMEM)
    return pl.pallas_call(
        forward_kernel,
        in_specs=[HBM] * 2,
        out_specs=[vm] * 5,
        out_shape=[jax.ShapeDtypeStruct(v, F32) for v in shapes],
        scratch_shapes=[
            pltpu.VMEM((12, 12, 4, 384), F32),
            pltpu.VMEM((VLOC, COLS), BF),
            pltpu.VMEM((72, 384), F32),
            pltpu.VMEM((8, PADDED), F32),
            pltpu.SemaphoreType.DMA,
            pltpu.SemaphoreType.DMA((len(ROW_CHUNKS),)),
        ],
        compiler_params=pltpu.CompilerParams(vmem_limit_bytes=BIG),
        cost_estimate=pl.CostEstimate(flops=2 * 8 * VLOC * COLS, bytes_accessed=9_500_000, transcendentals=0),
        name="forward",
    )(field, factor)


def join_kernel(wait_ref, msg_ref, y1_ref, y2_ref, level_ref, rest_ref):
    level_ref[...] = msg_ref[:, :SEP] + y1_ref[:, :SEP]
    rest_ref[...] = msg_ref[:, SEP : LEVELS * SEP] + y1_ref[:, SEP : LEVELS * SEP]


def join(wait, msg, y1, y2):
    vm = pl.BlockSpec(memory_space=pltpu.VMEM)
    return pl.pallas_call(
        join_kernel,
        in_specs=[UNUSED, vm, vm, UNUSED],
        out_specs=[vm] * 2,
        out_shape=[
            jax.ShapeDtypeStruct((4, SEP), F32),
            jax.ShapeDtypeStruct((4, (LEVELS - 1) * SEP), F32),
        ],
        compiler_params=pltpu.CompilerParams(vmem_limit_bytes=MIDDLE),
        cost_estimate=pl.CostEstimate(flops=30_000, bytes_accessed=400_000, transcendentals=0),
        name="join",
    )(wait, msg, y1, y2)


def faces_kernel(wait_ref, x1_ref, x2_ref, y1_ref, y2_ref, m1_ref, m2_ref):
    gy_odd, gx_odd = parities()
    m1_ref[:, :FACE] = x1_ref[...]
    m2_ref[:, :FACE] = x2_ref[...]
    tail = LEVELS * SEP
    low_x = slice(0, 384)
    high_x = slice(FACE - 384, FACE)

    def corner(cols):
        one = y1_ref[:, tail + cols.start : tail + cols.stop]
        two = y2_ref[:, cols]
        return jnp.where(gy_odd, one, two), jnp.where(gy_odd, two, one)

    low, high = corner(low_x), corner(high_x)
    for k in range(2):
        cols = slice(FACE + 384 * k, FACE + 384 * k + 384)
        m1_ref[:, cols] = jnp.where(gx_odd, low[k], high[k])
        m2_ref[:, cols] = jnp.where(gx_odd, high[k], low[k])


def faces(wait, x1, x2, y1, y2):
    vm = pl.BlockSpec(memory_space=pltpu.VMEM)
    return pl.pallas_call(
        faces_kernel,
        in_specs=[UNUSED] + [vm] * 4,
        out_specs=[vm] * 2,
        out_shape=[jax.ShapeDtypeStruct((4, SLAB), F32)] * 2,
        compiler_params=pltpu.CompilerParams(vmem_limit_bytes=SMALL),
        cost_estimate=pl.CostEstimate(flops=100_000, bytes_accessed=300_000, transcendentals=0),
        name="faces",
    )(wait, x1, x2, y1, y2)


def tables_kernel(
    wait_ref, r_ref, sx_ref, sy_ref, dt_ref, lx_ref, ly_ref, lz_ref, a_ref, b_ref, zf_ref, zb_ref, rs_ref, xs_ref
):
    xs_ref[...] = jnp.zeros_like(xs_ref)
    for n in range(4):
        for x in range(12):
            xs_ref[n, 16 * x : 16 * x + 12, :] = r_ref[x, :, n, :]
    lane = lax.broadcasted_iota(jnp.int32, (8, 256), 1)
    sub = lax.broadcasted_iota(jnp.int32, (8, 256), 0)
    slab = lane // 16
    xpos = jnp.where(slab < 12, slab + 1, jnp.where(slab == 12, 0, jnp.where(slab == 13, 13, 99)))
    yrow = lane % 16
    ypos = jnp.where(yrow < 12, yrow + 1, jnp.where(yrow == 12, 0, jnp.where(yrow == 13, 13, 99)))
    inner = jnp.logical_and(sub >= 1, sub <= 6)

    def exact(a, b, dims):
        return lax.dot_general(a, b, dims, precision=lax.Precision.HIGHEST, preferred_element_type=F32)

    def expand(mat_ref, pos, keep):
        parts = []
        for e in range(2):
            pick = jnp.where(jnp.logical_and(pos == 6 * e + sub, keep), 1.0, 0.0)
            parts.append(exact(mat_ref[e], pick, TN))
        return jnp.concatenate(parts, axis=0)

    everything = sub >= 0
    ax = expand(sx_ref, xpos, everything)
    ay = expand(sy_ref, ypos, everything)
    for i in range(16):
        hi, lo = split(ax[i : i + 1, :] * ay)
        a_ref[0, 16 * i : 16 * i + 16, :] = hi
        a_ref[1, 16 * i : 16 * i + 16, :] = lo
    bx = expand(sx_ref, xpos, inner)
    by = expand(sy_ref, ypos, inner)
    full = jnp.concatenate([bx[i : i + 1, :] * by for i in range(16)], axis=0)
    hi, lo = split(full.T)
    b_ref[0] = hi
    b_ref[1] = lo

    row = lax.broadcasted_iota(jnp.int32, (256, 8), 0)
    col = lax.broadcasted_iota(jnp.int32, (256, 8), 1)

    def column(lam_ref, group):
        total = jnp.zeros((256, 8), F32)
        for e in range(2):
            total += jnp.where(group == 8 * e + col, lam_ref[e : e + 1, :], 0.0)
        return jnp.sum(total, axis=1, keepdims=True)

    lateral = column(lx_ref, row // 16) + column(ly_ref, row % 16)

    for g in range(2):
        pick = jnp.where(
            lax.broadcasted_iota(jnp.int32, (64, 256), 0)
            == lax.broadcasted_iota(jnp.int32, (64, 256), 1) // 8 + 32 * g,
            1.0,
            0.0,
        )
        mine = sub == lane % 8
        spread = exact(dt_ref[...], pick, (((1,), (0,)), ((), ())))
        depth = exact(lz_ref[...], pick, (((1,), (0,)), ((), ())))
        depth = jnp.sum(jnp.where(mine, depth, 0.0), axis=0, keepdims=True)
        rs_ref[:, 256 * g : 256 * g + 256] = 1.0 / (lateral + depth)
        z = lax.broadcasted_iota(jnp.int32, (256, 256), 0) + 128 * g
        c = lax.broadcasted_iota(jnp.int32, (256, 256), 1) // 8 + 32 * g
        w = z + 1 - 6 * c
        table = jnp.zeros((256, 256), F32)
        for k in range(8):
            line = jnp.sum(jnp.where(mine, spread[8 * k : 8 * k + 8], 0.0), axis=0, keepdims=True)
            table = jnp.where(w == k, line, table)
        hi, lo = split(table)
        zf_ref[0, g] = hi
        zf_ref[1, g] = lo
        mid = jnp.logical_and(w >= 1, w <= 6)
        zb_ref[0, g] = jnp.where(mid, hi.astype(F32), 0.0).astype(BF)
        zb_ref[1, g] = jnp.where(mid, lo.astype(F32), 0.0).astype(BF)


def tables(wait, field, sx, sy, dt, lx, ly, lz):
    vm = pl.BlockSpec(memory_space=pltpu.VMEM)
    return pl.pallas_call(
        tables_kernel,
        in_specs=[UNUSED] + [vm] * 7,
        out_specs=[vm] * 6,
        out_shape=[
            jax.ShapeDtypeStruct((2, 256, 256), BF),
            jax.ShapeDtypeStruct((2, 256, 256), BF),
            jax.ShapeDtypeStruct((2, 2, 256, 256), BF),
            jax.ShapeDtypeStruct((2, 2, 256, 256), BF),
            jax.ShapeDtypeStruct((256, 512), F32),
            jax.ShapeDtypeStruct((4, 224, 384), F32),
        ],
        compiler_params=pltpu.CompilerParams(vmem_limit_bytes=SMALL),
        cost_estimate=pl.CostEstimate(flops=1_000_000_000, bytes_accessed=2_000_000, transcendentals=0),
        name="tables",
    )(wait, field, sx, sy, dt, lx, ly, lz)


def shifted(left, right):
    pair = jnp.concatenate([left, right], axis=1)
    pair = jnp.concatenate([pair, jnp.zeros((4, 2 * SEP), F32)], axis=0)
    return pltpu.roll(pair, LEAF, 1)[:, SEP:]


def chunk_values(chunk, level_refs):
    if chunk:
        return shifted(level_refs[0][...], level_refs[1][...]).astype(BF)
    own, level = level_refs
    lane = lax.broadcasted_iota(jnp.int32, (4, 128), 1)
    rest = pltpu.roll(jnp.concatenate([level[...], jnp.zeros((4, SEP), F32)], axis=0), LEAF, 1)
    head = jnp.where(lane < LEAF, own[...], rest[:4, :128])
    head = jnp.concatenate([head, jnp.zeros((4, 128), F32)], axis=0)
    return jnp.concatenate([head, rest[:, 128:]], axis=1).astype(BF)


def schwarz_kernel(first, chunks, *refs):
    wait_ref, r_ref, y1_ref, y2_ref, m1_ref, m2_ref, a_ref, b_ref, zf_ref, zb_ref, rs_ref = refs[:11]
    refs = refs[11:]
    level_refs = refs[: len(chunks) + 1] if chunks else ()
    refs = refs[len(level_refs) :]
    if chunks:
        f_ref, out_ref, v_ref, x_ref, chunk_ref, sem = refs
        cols = pl.ds(chunks[0] * SEP, len(chunks) * SEP)
        copy = pltpu.make_async_copy(f_ref.at[:, cols], chunk_ref, sem)
        copy.start()
    else:
        out_ref, x_ref = refs
    schwarz_body(first, r_ref, y1_ref, y2_ref, m1_ref, m2_ref, a_ref, b_ref, zf_ref, zb_ref, rs_ref, out_ref, x_ref)
    if chunks:
        copy.wait()
        total = jnp.zeros((8, VLOC), F32)
        for k, chunk in enumerate(chunks):
            values = chunk_values(chunk, level_refs[k : k + 2])
            for h in range(0, SEP, SEP // 2):
                cols = slice(k * SEP + h, k * SEP + h + SEP // 2)
                total = total + dot(values[:, h : h + SEP // 2], chunk_ref[:, cols], NT)
        v_ref[:, :VLOC] = total
        v_ref[:, VLOC:] = jnp.zeros((8, 640 - VLOC), F32)


def schwarz_body(
    first, r_ref, y1_ref, y2_ref, m1_ref, m2_ref, a_ref, b_ref, zf_ref, zb_ref, rs_ref, out_ref, x_ref
):
    gy_odd, gx_odd = parities()
    tail = LEVELS * SEP
    for k in range(out_ref.shape[0]):
        n = first + k
        x_ref[k] = r_ref[n]
        for x in range(12):
            one = y1_ref[n : n + 1, tail + 384 * x : tail + 384 * x + 384]
            two = y2_ref[n : n + 1, 384 * x : 384 * x + 384]
            x_ref[k, 16 * x + 12 : 16 * x + 13, :] = jnp.where(gy_odd, one, two)
            x_ref[k, 16 * x + 13 : 16 * x + 14, :] = jnp.where(gy_odd, two, one)
        for j in range(14):
            one = m1_ref[n : n + 1, 384 * j : 384 * j + 384]
            two = m2_ref[n : n + 1, 384 * j : 384 * j + 384]
            x_ref[k, 192 + j : 193 + j, :] = jnp.where(gx_odd, one, two)
            x_ref[k, 208 + j : 209 + j, :] = jnp.where(gx_odd, two, one)
        a = (a_ref[0][:, :224], a_ref[1][:, :224])
        t1 = split(dot3(a, split(x_ref[k])))
        backs = []
        for g in range(2):
            part = (t1[0][:, 128 * g : 128 * g + 256], t1[1][:, 128 * g : 128 * g + 256])
            t2 = dot3(part, (zf_ref[0, g], zf_ref[1, g]))
            t3 = split(t2 * rs_ref[:, 256 * g : 256 * g + 256])
            backs.append(dot3(t3, (zb_ref[0, g], zb_ref[1, g]), NT))
        t4 = split(
            jnp.concatenate(
                [backs[0][:, :128], backs[0][:, 128:] + backs[1][:, :128], backs[1][:, 128:]], axis=1
            )
        )
        out_ref[k] = dot3((b_ref[0][:192], b_ref[1][:192]), t4)


def schwarz(first, wait, chunks, levels, factor, field, y1, y2, m1, m2, tabs):
    vm = pl.BlockSpec(memory_space=pltpu.VMEM)
    kernel = lambda *refs: schwarz_kernel(first, chunks, *refs)
    extra = (*levels, factor) if chunks else ()
    out = jax.ShapeDtypeStruct((1, 192, 384), F32)
    scratch = [pltpu.VMEM((1, 224, 384), F32)]
    if chunks:
        scratch += [pltpu.VMEM((VLOC, len(chunks) * SEP), BF), pltpu.SemaphoreType.DMA]
    return pl.pallas_call(
        kernel,
        in_specs=[UNUSED] + [vm] * 10 + ([vm] * len(levels) + [HBM] if chunks else []),
        out_specs=[vm, vm] if chunks else vm,
        out_shape=[out, jax.ShapeDtypeStruct((8, 640), F32)] if chunks else out,
        scratch_shapes=scratch,
        compiler_params=pltpu.CompilerParams(vmem_limit_bytes=MIDDLE),
        cost_estimate=pl.CostEstimate(flops=900_000_000, bytes_accessed=700_000, transcendentals=0),
        name="schwarz",
    )(wait, field, y1, y2, m1, m2, *tabs, *extra)


PACK_LAST = SEP
PACK_PZ = PACK_LAST + 128
PACK_TILE = PACK_PZ + 384
PACK_V = PACK_TILE + 128
PACK = PACK_V + 640


def pack_kernel(*refs):
    l5_ref, l6_ref, *vertex_refs, const_ref, f_ref, pack_ref, chunk_ref, narrow_ref, sems = refs
    pairs = [
        (f_ref.at[:, pl.ds(5 * SEP, SEP)], chunk_ref),
        (f_ref.at[:, pl.ds(LEVELS * SEP, LEAF)], narrow_ref),
        (f_ref.at[:, pl.ds(6 * SEP, SEP)], pack_ref.at[:, pl.ds(0, SEP)]),
        (const_ref, pack_ref.at[:, pl.ds(PACK_PZ, 512)]),
    ]
    copies = []
    for k, (src, dst) in enumerate(pairs):
        copies.append(pltpu.make_async_copy(src, dst, sems.at[k]))
        copies[-1].start()
    values = shifted(l5_ref[...], l6_ref[...]).astype(BF)
    copies[0].wait()
    v = dot(values[:, : SEP // 2], chunk_ref[:, : SEP // 2], NT)
    v = v + dot(values[:, SEP // 2 :], chunk_ref[:, SEP // 2 :], NT)
    v = jnp.concatenate([v, jnp.zeros((8, 640 - VLOC), F32)], axis=1)
    v = v + sum(ref[...] for ref in vertex_refs)
    for k in range(3):
        term = v.astype(BF)
        v = v - term.astype(F32)
        pack_ref[16 * k : 16 * k + 16, PACK_V:] = jnp.concatenate([term, jnp.zeros((8, 640), BF)], axis=0)
    end = jnp.concatenate([l6_ref[:, SEP - 128 :], jnp.zeros((12, 128), F32)], axis=0)
    end = pltpu.roll(end, LEAF, 1)
    pack_ref[48:64, PACK_V : PACK_V + 128] = end.astype(BF)
    copies[1].wait()
    pack_ref[:, PACK_LAST : PACK_LAST + LEAF] = narrow_ref[...]
    pack_ref[:, PACK_LAST + LEAF : PACK_PZ] = jnp.zeros((VLOC, 128 - LEAF), BF)
    copies[2].wait()
    copies[3].wait()


def packed(l5, l6, vertex, factor):
    pz = np.zeros((128, 384), np.float32)
    pz[:65] = line_table(prolong_np, 64).T
    hi, lo = split_np(pz)
    const = np.zeros((VLOC, 512), ml_dtypes.bfloat16)
    const[:128, :384] = hi
    const[128:256, :384] = lo
    for ab in range(9):
        for c in range(65):
            const[ab * 65 + c, 384 + c] = 1
    vm = pl.BlockSpec(memory_space=pltpu.VMEM)
    return pl.pallas_call(
        pack_kernel,
        in_specs=[vm] * (2 + len(vertex)) + [HBM] * 2,
        out_specs=vm,
        out_shape=jax.ShapeDtypeStruct((VLOC, PACK), BF),
        scratch_shapes=[
            pltpu.VMEM((VLOC, SEP), BF),
            pltpu.VMEM((VLOC, LEAF), BF),
            pltpu.SemaphoreType.DMA((4,)),
        ],
        compiler_params=pltpu.CompilerParams(vmem_limit_bytes=MIDDLE),
        cost_estimate=pl.CostEstimate(flops=2 * 8 * VLOC * SEP, bytes_accessed=4_000_000, transcendentals=0),
        name="pack",
    )(l5, l6, *vertex, jnp.asarray(const), factor)


def late_kernel(mine_ref, got_ref, pack_ref, s_ref, out_ref):
    top = jnp.concatenate([mine_ref[...] + got_ref[...], jnp.zeros((4, SEP), F32)], axis=0)
    top = pltpu.roll(jnp.concatenate([top, jnp.zeros((8, 128), F32)], axis=1), LEAF, 1)
    lane = lax.broadcasted_iota(jnp.int32, (8, 128), 1)
    head = jnp.where(lane < LEAF, pack_ref[48:64, PACK_V : PACK_V + 128][:8].astype(F32), top[:, :128])
    nv = jnp.concatenate([head, top[:, 128:]], axis=1).astype(BF)
    add = dot(nv[:, : SEP // 2], pack_ref[:, : SEP // 2], NT)
    add = add + dot(nv[:, SEP // 2 :], pack_ref[:, SEP // 2 : PACK_PZ], NT)
    v = jnp.concatenate([add, jnp.zeros((8, 640 - VLOC), F32)], axis=1)
    for k in range(3):
        v = v + pack_ref[32 - 16 * k : 48 - 16 * k, PACK_V:][:8].astype(F32)
    spread = jnp.where(ab_mask(72, 640), jnp.concatenate([v] * 9, axis=0), 0.0)
    hi, lo = split(spread)
    tile = pack_ref[:, PACK_TILE:PACK_V]
    vert = dot(hi[:, :VLOC], tile) + dot(lo[:, :VLOC], tile)
    tables = (pack_ref[:128, PACK_PZ:PACK_TILE], pack_ref[128:256, PACK_PZ:PACK_TILE])
    lines = dot3(split(vert), tables)
    p0 = [float(q) for q in prolong_np[0]]
    p1 = [float(q) for q in prolong_np[1]]
    for y in range(12):
        b, j = divmod(y, 6)
        planes = []
        for a in range(3):
            low = lines[(a * 3 + b) * 8 : (a * 3 + b) * 8 + 4, :]
            high = lines[(a * 3 + b + 1) * 8 : (a * 3 + b + 1) * 8 + 4, :]
            planes.append(p0[j] * low + p1[j] * high)
        for x in range(12):
            e, i = divmod(x, 6)
            out_ref[x, y] = s_ref[x, y] + (p0[i] * planes[e] + p1[i] * planes[e + 1])


def late(mine, got, pack, solved):
    vm = pl.BlockSpec(memory_space=pltpu.VMEM)
    return pl.pallas_call(
        late_kernel,
        in_specs=[vm] * 4,
        out_specs=vm,
        out_shape=jax.ShapeDtypeStruct((12, 12, 4, 384), F32),
        compiler_params=pltpu.CompilerParams(vmem_limit_bytes=SMALL),
        cost_estimate=pl.CostEstimate(flops=2 * 8 * VLOC * SEP, bytes_accessed=5_000_000, transcendentals=0),
        name="late",
    )(mine, got, pack, solved)


def exchange(value, mask):
    return lax.ppermute(value, ("gx", "gy"), [(i, i ^ mask) for i in range(128)])


def odd_pairs(value, axis):
    count = lax.axis_size(axis)
    return lax.ppermute(value, axis, [(i, (i + 1) % count if i % 2 else (i - 1) % count) for i in range(count)])


MASKS = (1, 3, 4, 12, 16, 32, 96)


def local(residual, sx, sy, depth_vectors, lam_x, lam_y, lam_z, coarse_factor):
    factor = coarse_factor.reshape(VLOC, COLS)
    field = residual.transpose(1, 2, 0, 3)
    msg, own, y2, x1, x2 = forward(field, factor)
    got1 = exchange(msg, 1)
    dt = depth_vectors.transpose(1, 2, 0).reshape(64, 64)
    tabs = tables(own, field, sx, sy, dt, lam_x, lam_y, lam_z.transpose(1, 0))
    got2 = odd_pairs(y2, "gy")
    level, sep = join(tabs[4], msg, got1, got2)
    done = [own, level]
    for mask in MASKS[1:-1]:
        sep = sep + exchange(sep, mask)
        done.append(sep[:, :SEP])
        sep = sep[:, SEP:]
    got = exchange(sep, MASKS[-1])
    m1, m2 = faces(done[FACES_AFTER], x1, x2, got1, got2)
    m1 = exchange(m1, 16)
    m2 = odd_pairs(m2, "gx")
    parts = []
    vertex = []
    for n, (level, chunks) in enumerate(WORK):
        levels = done[chunks[0] : chunks[-1] + 2] if chunks else ()
        part = schwarz(n, done[level], chunks, levels, factor, tabs[5], got1, got2, m1, m2, tabs[:5])
        if chunks:
            part, more = part
            vertex.append(more)
        parts.append(part)
    pack = packed(done[5], done[6], vertex, factor)
    solved = jnp.concatenate(parts, axis=0).reshape(4, 12, 16, 384)[:, :, :12].transpose(1, 2, 0, 3)
    out = late(sep, got, pack, solved)
    return out.transpose(2, 0, 1, 3)


FACES_AFTER = 1
WORK = ((2, (0, 1)), (3, (2,)), (4, ()), (5, (3, 4)))


def solution(mesh):
    return jax.shard_map(
        local,
        mesh=mesh,
        in_specs=(
            P(None, "gx", "gy", None),
            P("gx", None, None),
            P("gy", None, None),
            P(),
            P("gx", None),
            P("gy", None),
            P(),
            P("gx", "gy", None, None),
        ),
        out_specs=P(None, "gx", "gy", None),
        check_vma=False,
    )
```
